512 devices in a mesh: rows: 128 (over x, y_hi, z), snap: 4 (over y_lo, core).
Axes of the slice: x: 4, y: 4 (y_hi: 2, y_lo: 2; y = y_hi * 2 + y_lo), z: 16, core: 2. Of those that a mesh axis runs over, the one named last changes fastest.
Arguments:
- snapshots: float32 [98304, 2048], P('rows', 'snap'), may hold values from -5000 to 5000
Outputs:
- correlation: float32 [2048, 2048], P('snap', 'rows')
The draws below stay inside these ranges and needn't reach their ends.
All inputs are finite; a program needn't handle non-finite values.
Results may differ from the reference program's by a relative error of at most 0.00026.
Values sent between devices are 32-bit elements; how exact they have to be, the bound alone decides.
A program may use at most 64 MiB of HBM per device.

```python
import math
import jax
import jax.numpy as jnp
from jax import lax

NSNAP = 2048
ROWS = 98304


def draw_snapshots(key, part):
    key = jax.random.fold_in(key, 11)
    key_list = jax.random.split(key, 5)
    position = jnp.arange(ROWS, dtype=jnp.float32)
    row_ramp = 1.0 + 2.0 * position / max(ROWS - 1, 1)
    col_scale = jnp.exp(jax.random.uniform(key_list[1], (1, NSNAP), jnp.float32, 0.0, math.log(10.0)))
    mode_count = max(NSNAP // 4, 8)
    spectrum_total = 0.0
    for number in range(1, mode_count + 1):
        spectrum_total = spectrum_total + number ** (-0.5)
    mode_index = jnp.arange(1, mode_count + 1, dtype=jnp.float32)
    mode_gain = mode_index ** (-0.25) / math.sqrt(spectrum_total)
    spatial = jax.random.truncated_normal(key_list[2], -4.0, 4.0, (ROWS, mode_count), jnp.float32)
    temporal = jax.random.truncated_normal(key_list[3], -4.0, 4.0, (mode_count, NSNAP), jnp.float32) * mode_gain[:, None]
    mode_part = jnp.dot(spatial, temporal, precision=lax.Precision.HIGHEST, preferred_element_type=jnp.float32)
    mean_part = 1.5 * jax.random.truncated_normal(key_list[0], -4.0, 4.0, (ROWS, 1), jnp.float32)
    noise_part = 0.6 * jax.random.truncated_normal(key_list[4], -4.0, 4.0, (ROWS, NSNAP), jnp.float32)
    return mean_part + row_ramp[:, None] * col_scale * (mode_part + noise_part)


def setup_inputs(seed: int = 0) -> dict:
    streams_of = jax.random.split(jax.random.key(seed), 2)
    return {
        "snapshots": draw_snapshots(jax.random.fold_in(streams_of[1], 71), 0),
    }


eps = 1e-06

def reference(snapshots):
    mean_flow = lax.optimization_barrier(jnp.sum(snapshots, axis=1, keepdims=True)) / NSNAP
    fluctuation = snapshots - mean_flow
    gram = lax.dot_general(fluctuation, fluctuation, (((0,), (0,)), ((), ())), precision=lax.Precision.HIGHEST, preferred_element_type=jnp.float32)
    energy = lax.optimization_barrier(jnp.sum(fluctuation * fluctuation, axis=0))
    scaling = lax.rsqrt(energy + eps)
    return gram * scaling[:, None] * scaling[None, :]
```

```python
import jax
import jax.numpy as jnp
from jax import lax
from jax.experimental import pallas as pl
from jax.experimental.pallas import tpu as pltpu
from jax.sharding import PartitionSpec as P

eps = 1e-06
MESH = pl.DeviceIdType.MESH
f32, bf16 = jnp.float32, jnp.bfloat16

NX, NH, NZ = 4, 2, 16
ROWS, COLS = 768, 512
HALF = ROWS // 2
TILE = 128
SNAPS = 2048
ZR, ZL = NZ // 2, NZ // 2 - 1


def device(x, h, z, low, core):
    return ((x * NH + h) * NZ + z, low * 2 + core)


def kernel(
    x_ref, out_ref,
    other, cross, sums, mean, hi, lo, t_hi, t_lo, c_hi, c_lo,
    aa, ab, unit, from_left, from_right,
    unit_r, unit_l, ab_r, ab_l,
    e_own, e_r, e_l, e_x, e_sum, e_h, e_all, e_col,
    held, flip, direct, turned,
    core_ss, core_rs, y_ss, y_rs, relay_ss, relay_rs, sum_ss, sum_rs,
    xr_ss, xr_rs, xl_ss, xl_rs,
    ur_ss, ur_rs, ul_ss, ul_rs, abr_ss, abr_rs, abl_ss, abl_rs,
    er_ss, er_rs, el_ss, el_rs, ex_ss, ex_rs, eh_ss, eh_rs, eg_ss, eg_rs,
    fin_ss, fin_rs,
):
    r, s = lax.axis_index("rows"), lax.axis_index("snap")
    x, h, z = r // (NH * NZ), (r // NZ) % NH, r % NZ
    low, core = s // 2, s % 2
    zr, zl = device(x, h, (z + 1) % NZ, low, core), device(x, h, (z + NZ - 1) % NZ, low, core)
    xr, xl = device((x + 1) % NX, h, z, low, core), device((x + NX - 1) % NX, h, z, low, core)
    xx = device((x + 2) % NX, h, z, low, core)
    hh = device(x, 1 - h, z, low, core)
    twin = device(x, h, z, low, 1 - core)
    pair = device(x, h, z, 1 - low, core)
    diagonal = device(x, h, z, 1 - low, 1 - core)
    group = (twin, pair, diagonal)
    pending = []

    def send(src, dst, send_sem, recv_sem, target):
        copy = pltpu.make_async_remote_copy(
            src_ref=src, dst_ref=dst, send_sem=send_sem, recv_sem=recv_sem,
            device_id=target, device_id_type=MESH,
        )
        copy.start()
        pending.append((src, send_sem))
        return copy

    def arrived(dst, sem):
        pltpu.make_async_copy(dst, dst, sem).wait()

    barrier = pltpu.get_barrier_semaphore()
    near = (twin, pair, diagonal, zr, zl, xr, xl, xx, hh)
    for target in near:
        pl.semaphore_signal(barrier, inc=1, device_id=target, device_id_type=MESH)

    for q in range(ROWS // TILE):
        block = x_ref[q * TILE:(q + 1) * TILE, :]
        part = block[:, 0:128] + block[:, 128:256] + block[:, 256:384] + block[:, 384:512]
        sums[s, q:q + 1, :] = jnp.sum(part.T, axis=0, keepdims=True)
    sums[s, 6:8, :] = jnp.zeros((2, TILE), f32)
    pl.semaphore_wait(barrier, len(near))

    for i, target in enumerate(group):
        send(sums.at[s], sums.at[s], sum_ss.at[i], sum_rs.at[i], target)
    send(x_ref, other, core_ss, core_rs, twin)
    give = pl.multiple_of((1 - low) * HALF, HALF)
    send(x_ref.at[pl.ds(give, HALF)], cross.at[0], y_ss, y_rs, pair)

    for i, d in enumerate((s ^ 1, s ^ 2, s ^ 3)):
        arrived(sums.at[d], sum_rs.at[i])
    mean_rows = (sums[0] + sums[1] + sums[2] + sums[3]) / SNAPS
    for q in range(ROWS // TILE):
        wide = jnp.broadcast_to(mean_rows[q:q + 1, :], (TILE, TILE))
        mean[q * TILE:(q + 1) * TILE, :] = wide.T

    def split(value):
        high = value.astype(bf16)
        return high, (value - high.astype(f32)).astype(bf16)

    def turn(block, q, to_hi, to_lo, j):
        high, rest = split(block.T)
        to_hi[j * TILE:(j + 1) * TILE, pl.ds(q * TILE, TILE)] = high
        to_lo[j * TILE:(j + 1) * TILE, pl.ds(q * TILE, TILE)] = rest

    energy = [jnp.zeros((8, TILE), f32) for _ in range(4)]
    for q in range(ROWS // TILE):
        rows = slice(q * TILE, (q + 1) * TILE)
        for j in range(4):
            block = x_ref[rows, j * TILE:(j + 1) * TILE] - mean[rows, :]
            energy[j] += jnp.sum((block * block).reshape(TILE // 8, 8, TILE), axis=0)
            high, rest = split(block)
            hi[rows, j * TILE:(j + 1) * TILE] = high
            lo[rows, j * TILE:(j + 1) * TILE] = rest
            turn(block, q, t_hi.at[0], t_lo.at[0], j)
    for j in range(4):
        e_own[j:j + 1, :] = jnp.sum(energy[j], axis=0, keepdims=True)
    e_own[4:8, :] = jnp.zeros((4, TILE), f32)

    def e_step(t):
        if t > 0:
            arrived(e_r.at[t - 1], er_rs.at[t - 1])
        if t < ZR:
            send(e_own if t == 0 else e_r.at[t - 1], e_r.at[t], er_ss.at[t], er_rs.at[t], zr)
        if 0 < t <= ZL:
            arrived(e_l.at[t - 1], el_rs.at[t - 1])
        if t < ZL:
            send(e_own if t == 0 else e_l.at[t - 1], e_l.at[t], el_ss.at[t], el_rs.at[t], zl)

    e_step(0)

    def product(a_hi, a_lo, b_hi, b_lo):
        total = jnp.dot(a_hi, b_hi, preferred_element_type=f32)
        total += jnp.dot(a_hi, b_lo, preferred_element_type=f32)
        return total + jnp.dot(a_lo, b_hi, preferred_element_type=f32)

    def own_chip(side, owner):
        @pl.loop(0, 2)
        def _(half):
            at = pl.ds(pl.multiple_of(half * 256, 256), 256)
            got = product(t_hi[side, at, :], t_lo[side, at, :], hi[...], lo[...])
            aa[owner * 2 + half] = got.reshape(NZ, 16, COLS)

    own_chip(0, core)
    arrived(other, core_rs)
    for q in range(ROWS // TILE):
        rows = slice(q * TILE, (q + 1) * TILE)
        for j in range(4):
            turn(other[rows, j * TILE:(j + 1) * TILE] - mean[rows, :], q, t_hi.at[1], t_lo.at[1], j)
    own_chip(1, 1 - core)

    a_half, b_half = pl.ds(0, ZR), pl.ds(ZR, ZR)
    far, right, left = (x + 2) % NX, (x + 1) % NX, (x + NX - 1) % NX
    send(aa.at[far, a_half], from_left.at[0], xr_ss.at[0], xr_rs.at[0], xr)
    send(aa.at[far, b_half], from_right.at[0], xl_ss.at[0], xl_rs.at[0], xl)
    send(aa.at[right, b_half], from_left.at[1], xr_ss.at[1], xr_rs.at[1], xr)
    send(aa.at[left, a_half], from_right.at[1], xl_ss.at[1], xl_rs.at[1], xl)
    for t in range(1, 4):
        e_step(t)
    arrived(from_left.at[0], xr_rs.at[0])
    from_left[0] = from_left[0] + aa[right, a_half]
    send(from_left.at[0], from_left.at[2], xr_ss.at[2], xr_rs.at[2], xr)
    arrived(from_right.at[0], xl_rs.at[0])
    from_right[0] = from_right[0] + aa[left, b_half]
    send(from_right.at[0], from_right.at[2], xl_ss.at[2], xl_rs.at[2], xl)
    for t in range(4, ZR + 1):
        e_step(t)
    e_x[3] = e_own[...] + jnp.sum(e_r[...], axis=0) + jnp.sum(e_l[...], axis=0)
    for i, target in enumerate((xr, xl, xx)):
        send(e_x.at[3], e_x.at[i], ex_ss.at[i], ex_rs.at[i], target)

    keep = pl.multiple_of(low * HALF, HALF)

    def cross_chip(side):
        for q in range(HALF // TILE):
            rows = slice(q * TILE, (q + 1) * TILE)
            level = mean[pl.ds(keep + q * TILE, TILE), :]
            for j in range(4):
                turn(cross[side, rows, j * TILE:(j + 1) * TILE] - level, q, c_hi.at[side], c_lo.at[side], j)

        @pl.loop(0, 4)
        def _(tile):
            at = pl.ds(pl.multiple_of(tile * TILE, TILE), TILE)
            got = product(c_hi[side, at, :], c_lo[side, at, :],
                          hi[pl.ds(keep, HALF), :], lo[pl.ds(keep, HALF), :])
            for j in range(4):
                ab[side, tile * 4 + j] = got[:, j * TILE:(j + 1) * TILE]

    def z_step(t, part, slots_r, slots_l, ssr, rsr, ssl, rsl):
        to_r, to_l = (z + ZR - t + NZ) % NZ, (z + NZ - ZL + t) % NZ
        if 0 < t < ZR:
            arrived(slots_r.at[t - 1], rsr.at[t - 1])
            slots_r[t - 1] = slots_r[t - 1] + part[to_r]
        if t < ZR:
            src = part.at[to_r] if t == 0 else slots_r.at[t - 1]
            send(src, slots_r.at[t], ssr.at[t], rsr.at[t], zr)
        if 0 < t < ZL:
            arrived(slots_l.at[t - 1], rsl.at[t - 1])
            slots_l[t - 1] = slots_l[t - 1] + part[to_l]
        if t < ZL:
            src = part.at[to_l] if t == 0 else slots_l.at[t - 1]
            send(src, slots_l.at[t], ssl.at[t], rsl.at[t], zl)

    def z_last(part, slots_r, slots_l, rsr, rsl):
        arrived(slots_r.at[ZR - 1], rsr.at[ZR - 1])
        arrived(slots_l.at[ZL - 1], rsl.at[ZL - 1])
        return part[z] + slots_r[ZR - 1] + slots_l[ZL - 1]

    def unit_step(t):
        z_step(t, unit, unit_r, unit_l, ur_ss, ur_rs, ul_ss, ul_rs)

    def cross_step(t, side):
        z_step(t, ab.at[side], ab_r.at[side], ab_l.at[side],
               abr_ss.at[side], abr_rs.at[side], abl_ss.at[side], abl_rs.at[side])

    arrived(cross.at[0], y_rs)
    send(cross.at[0], cross.at[1], relay_ss, relay_rs, twin)
    cross_chip(0)
    cross_step(0, 0)

    arrived(from_left.at[1], xr_rs.at[1])
    arrived(from_right.at[1], xl_rs.at[1])
    arrived(from_left.at[2], xr_rs.at[2])
    arrived(from_right.at[2], xl_rs.at[2])
    unit[a_half] = aa[x, a_half] + from_left[2] + from_right[1]
    unit[b_half] = aa[x, b_half] + from_left[1] + from_right[2]
    unit_step(0)

    arrived(cross.at[1], relay_rs)
    cross_chip(1)
    cross_step(0, 1)

    for i in range(3):
        arrived(e_x.at[i], ex_rs.at[i])
    e_sum[...] = e_x[0] + e_x[1] + e_x[2] + e_x[3]
    send(e_sum, e_h, eh_ss, eh_rs, hh)
    for t in range(1, 3):
        cross_step(t, 0)
        unit_step(t)
        cross_step(t, 1)
    arrived(e_h, eh_rs)
    e_all[s] = e_sum[...] + e_h[...]
    for i, target in enumerate(group):
        send(e_all.at[s], e_all.at[s], eg_ss.at[i], eg_rs.at[i], target)
    for t in range(3, ZR):
        cross_step(t, 0)
        unit_step(t)
        cross_step(t, 1)
    for i, d in enumerate((s ^ 1, s ^ 2, s ^ 3)):
        arrived(e_all.at[d], eg_rs.at[i])

    held[...] = z_last(unit, unit_r, unit_l, ur_rs, ul_rs)
    to_x, to_h = 2 * low + x // 2, x % 2
    mine = jnp.logical_and(to_x == x, to_h == h)

    @pl.when(mine)
    def _():
        pltpu.make_async_copy(held, direct.at[h], fin_rs.at[0]).start()

    @pl.when(jnp.logical_not(mine))
    def _():
        pltpu.make_async_remote_copy(
            src_ref=held, dst_ref=direct.at[h], send_sem=fin_ss.at[0], recv_sem=fin_rs.at[0],
            device_id=device(to_x, to_h, z, low, core), device_id_type=MESH,
        ).start()

    row_tile, lane_tile = z // 4, z % 4
    me = x * NH + h
    for side in range(2):
        block = z_last(ab.at[side], ab_r.at[side], ab_l.at[side], abr_rs.at[side], abl_rs.at[side])
        flip[side, 0] = block
        flip[side, 1] = block.T
        their = core if side == 0 else 1 - core

        @pl.loop(0, 8)
        def _(k):
            src = pl.ds(pl.multiple_of(k * 16, 16), 16)
            lanes = pl.ds(pl.multiple_of(lane_tile * TILE, TILE), TILE)
            ox, oh, oz = 2 * (1 - low) + their, row_tile // 2, (row_tile % 2) * 8 + k
            own = jnp.logical_and(ox == x, jnp.logical_and(oh == h, oz == z))

            @pl.when(own)
            def _():
                pltpu.make_async_copy(flip.at[side, 0, src], direct.at[me, :, lanes], fin_rs.at[0]).start()

            @pl.when(jnp.logical_not(own))
            def _():
                pltpu.make_async_remote_copy(
                    src_ref=flip.at[side, 0, src], dst_ref=direct.at[me, :, lanes],
                    send_sem=fin_ss.at[1 + side * 16 + k], recv_sem=fin_rs.at[0],
                    device_id=device(ox, oh, oz, low, core), device_id_type=MESH,
                ).start()

            wide = pl.ds(pl.multiple_of(row_tile * TILE, TILE), TILE)
            pltpu.make_async_remote_copy(
                src_ref=flip.at[side, 1, src], dst_ref=turned.at[me, :, wide],
                send_sem=fin_ss.at[9 + side * 16 + k], recv_sem=fin_rs.at[1],
                device_id=device(2 * low + core, lane_tile // 2, (lane_tile % 2) * 8 + k, 1 - low, their),
                device_id_type=MESH,
            ).start()

    line = h * 2 + z // 8
    e_col[...] = jnp.broadcast_to(e_all[x, pl.ds(line, 1), :], (TILE, TILE)).T
    scale_j = lax.rsqrt(e_col[pl.ds(pl.multiple_of((z % 8) * 16, 16), 16), :] + eps)
    scale_i = lax.rsqrt(e_all[s] + eps)

    def finish(total):
        for j in range(4):
            lanes = slice(j * TILE, (j + 1) * TILE)
            out_ref[:, lanes] = total[:, lanes] * scale_i[j:j + 1, :] * scale_j

    @pl.when(x // 2 == low)
    def _():
        arrived(direct.at[pl.ds(0, 2)], fin_rs.at[0])
        finish(direct[0] + direct[1])

    @pl.when(x // 2 != low)
    def _():
        arrived(direct, fin_rs.at[0])
        arrived(turned, fin_rs.at[1])
        finish(jnp.sum(direct[...], axis=0) + jnp.sum(turned[...], axis=0))

    for src, sem in pending:
        arrived(src, sem)

    @pl.when(jnp.logical_not(mine))
    def _():
        arrived(held, fin_ss.at[0])

    for side in range(2):
        their = core if side == 0 else 1 - core

        @pl.loop(0, 8)
        def _(k):
            src = flip.at[side, 0, pl.ds(0, 16)]
            ox, oh, oz = 2 * (1 - low) + their, row_tile // 2, (row_tile % 2) * 8 + k
            own = jnp.logical_and(ox == x, jnp.logical_and(oh == h, oz == z))

            @pl.when(jnp.logical_not(own))
            def _():
                arrived(src, fin_ss.at[1 + side * 16 + k])

            arrived(src, fin_ss.at[9 + side * 16 + k])


def per_device(snapshots):
    dma = pltpu.SemaphoreType.DMA
    vmem = pltpu.VMEM
    strip = pl.pallas_call(
        kernel,
        out_shape=jax.ShapeDtypeStruct((16, COLS), f32),
        in_specs=[pl.BlockSpec(memory_space=pltpu.VMEM)],
        out_specs=pl.BlockSpec(memory_space=pltpu.VMEM),
        scratch_shapes=[
            vmem((ROWS, COLS), f32),
            vmem((2, HALF, COLS), f32),
            vmem((4, 8, TILE), f32),
            vmem((ROWS, TILE), f32),
            vmem((ROWS, COLS), bf16), vmem((ROWS, COLS), bf16),
            vmem((2, COLS, ROWS), bf16), vmem((2, COLS, ROWS), bf16),
            vmem((2, COLS, HALF), bf16), vmem((2, COLS, HALF), bf16),
            vmem((4, NZ, 16, COLS), f32),
            vmem((2, NZ, TILE, TILE), f32),
            vmem((NZ, 16, COLS), f32),
            vmem((3, ZR, 16, COLS), f32), vmem((3, ZR, 16, COLS), f32),
            vmem((ZR, 16, COLS), f32), vmem((ZL, 16, COLS), f32),
            vmem((2, ZR, TILE, TILE), f32), vmem((2, ZL, TILE, TILE), f32),
            vmem((8, TILE), f32), vmem((ZR, 8, TILE), f32), vmem((ZL, 8, TILE), f32),
            vmem((4, 8, TILE), f32), vmem((8, TILE), f32), vmem((8, TILE), f32),
            vmem((4, 8, TILE), f32), vmem((TILE, TILE), f32),
            vmem((16, COLS), f32), vmem((2, 2, TILE, TILE), f32),
            vmem((8, 16, COLS), f32), vmem((8, 16, COLS), f32),
            dma, dma, dma, dma, dma, dma, dma((3,)), dma((3,)),
            dma((3,)), dma((3,)), dma((3,)), dma((3,)),
            dma((ZR,)), dma((ZR,)), dma((ZL,)), dma((ZL,)),
            dma((2, ZR)), dma((2, ZR)), dma((2, ZL)), dma((2, ZL)),
            dma((ZR,)), dma((ZR,)), dma((ZL,)), dma((ZL,)),
            dma((3,)), dma((3,)), dma, dma, dma((3,)), dma((3,)),
            dma((33,)), dma((2,)),
        ],
        compiler_params=pltpu.CompilerParams(
            collective_id=0, has_side_effects=True, vmem_limit_bytes=48 << 20
        ),
        cost_estimate=pl.CostEstimate(flops=3_600_000_000, bytes_accessed=1_700_000, transcendentals=0),
        name="gram",
    )(snapshots)
    return strip.T


def solution(mesh):
    return jax.shard_map(
        per_device, mesh=mesh, in_specs=(P("rows", "snap"),), out_specs=P("snap", "rows"), check_vma=False
    )
```

```python
import jax
import jax.numpy as jnp
from jax import lax
from jax.experimental import pallas as pl
from jax.experimental.pallas import tpu as pltpu
from jax.sharding import PartitionSpec as P

eps = 1e-06
MESH = pl.DeviceIdType.MESH
f32, bf16 = jnp.float32, jnp.bfloat16

NX, NH, NZ = 4, 2, 16
ROWS, COLS = 768, 512
HALF = ROWS // 2
TILE = 128
SNAPS = 2048
ZR, ZL = NZ // 2, NZ // 2 - 1


def device(x, h, z, low, core):
    return ((x * NH + h) * NZ + z, low * 2 + core)


def kernel(
    x_ref, out_ref,
    other, cross, sums, mean, hi, lo, t_hi, t_lo, c_hi, c_lo,
    aa, ab, unit, from_left, from_right,
    unit_r, unit_l, ab_r, ab_l,
    e_own, e_r, e_l, e_x, e_sum, e_h, e_all, e_col,
    held, flip, direct, turned,
    core_ss, core_rs, y_ss, y_rs, relay_ss, relay_rs, sum_ss, sum_rs,
    xr_ss, xr_rs, xl_ss, xl_rs,
    ur_ss, ur_rs, ul_ss, ul_rs, abr_ss, abr_rs, abl_ss, abl_rs,
    er_ss, er_rs, el_ss, el_rs, ex_ss, ex_rs, eh_ss, eh_rs, eg_ss, eg_rs,
    fin_ss, fin_rs,
):
    r, s = lax.axis_index("rows"), lax.axis_index("snap")
    x, h, z = r // (NH * NZ), (r // NZ) % NH, r % NZ
    low, core = s // 2, s % 2
    zr, zl = device(x, h, (z + 1) % NZ, low, core), device(x, h, (z + NZ - 1) % NZ, low, core)
    xr, xl = device((x + 1) % NX, h, z, low, core), device((x + NX - 1) % NX, h, z, low, core)
    xx = device((x + 2) % NX, h, z, low, core)
    hh = device(x, 1 - h, z, low, core)
    twin = device(x, h, z, low, 1 - core)
    pair = device(x, h, z, 1 - low, core)
    diagonal = device(x, h, z, 1 - low, 1 - core)
    group = (twin, pair, diagonal)
    pending = []

    def send(src, dst, send_sem, recv_sem, target):
        copy = pltpu.make_async_remote_copy(
            src_ref=src, dst_ref=dst, send_sem=send_sem, recv_sem=recv_sem,
            device_id=target, device_id_type=MESH,
        )
        copy.start()
        pending.append((src, send_sem))
        return copy

    def arrived(dst, sem):
        pltpu.make_async_copy(dst, dst, sem).wait()

    barrier = pltpu.get_barrier_semaphore()
    near = (twin, pair, diagonal, zr, zl, xr, xl, xx, hh)
    for target in near:
        pl.semaphore_signal(barrier, inc=1, device_id=target, device_id_type=MESH)

    for q in range(ROWS // TILE):
        block = x_ref[q * TILE:(q + 1) * TILE, :]
        part = block[:, 0:128] + block[:, 128:256] + block[:, 256:384] + block[:, 384:512]
        sums[s, q:q + 1, :] = jnp.sum(part.T, axis=0, keepdims=True)
    sums[s, 6:8, :] = jnp.zeros((2, TILE), f32)
    pl.semaphore_wait(barrier, len(near))

    for i, target in enumerate(group):
        send(sums.at[s], sums.at[s], sum_ss.at[i], sum_rs.at[i], target)
    send(x_ref, other, core_ss, core_rs, twin)
    give = pl.multiple_of((1 - low) * HALF, HALF)
    for e in range(2):
        for q in range(HALF // TILE):
            lanes = pl.ds(e * 256, 256)
            send(x_ref.at[pl.ds(give + q * TILE, TILE), lanes], cross.at[0, pl.ds(q * TILE, TILE), lanes],
                 y_ss.at[e, q], y_rs.at[e, q], pair)

    for i, d in enumerate((s ^ 1, s ^ 2, s ^ 3)):
        arrived(sums.at[d], sum_rs.at[i])
    mean_rows = (sums[0] + sums[1] + sums[2] + sums[3]) / SNAPS
    for q in range(ROWS // TILE):
        wide = jnp.broadcast_to(mean_rows[q:q + 1, :], (TILE, TILE))
        mean[q * TILE:(q + 1) * TILE, :] = wide.T

    def split(value):
        high = value.astype(bf16)
        return high, (value - high.astype(f32)).astype(bf16)

    def turn(block, q, to_hi, to_lo, j):
        high, rest = split(block.T)
        to_hi[j * TILE:(j + 1) * TILE, pl.ds(q * TILE, TILE)] = high
        to_lo[j * TILE:(j + 1) * TILE, pl.ds(q * TILE, TILE)] = rest

    energy = [jnp.zeros((8, TILE), f32) for _ in range(4)]
    for q in range(ROWS // TILE):
        rows = slice(q * TILE, (q + 1) * TILE)
        for j in range(4):
            block = x_ref[rows, j * TILE:(j + 1) * TILE] - mean[rows, :]
            energy[j] += jnp.sum((block * block).reshape(TILE // 8, 8, TILE), axis=0)
            high, rest = split(block)
            hi[rows, j * TILE:(j + 1) * TILE] = high
            lo[rows, j * TILE:(j + 1) * TILE] = rest
            turn(block, q, t_hi.at[0], t_lo.at[0], j)
    for j in range(4):
        e_own[j:j + 1, :] = jnp.sum(energy[j], axis=0, keepdims=True)
    e_own[4:8, :] = jnp.zeros((4, TILE), f32)

    def e_step(t):
        if t > 0:
            arrived(e_r.at[t - 1], er_rs.at[t - 1])
        if t < ZR:
            send(e_own if t == 0 else e_r.at[t - 1], e_r.at[t], er_ss.at[t], er_rs.at[t], zr)
        if 0 < t <= ZL:
            arrived(e_l.at[t - 1], el_rs.at[t - 1])
        if t < ZL:
            send(e_own if t == 0 else e_l.at[t - 1], e_l.at[t], el_ss.at[t], el_rs.at[t], zl)

    e_step(0)

    def product(a_hi, a_lo, b_hi, b_lo):
        total = jnp.dot(a_hi, b_hi, preferred_element_type=f32)
        total += jnp.dot(a_hi, b_lo, preferred_element_type=f32)
        return total + jnp.dot(a_lo, b_hi, preferred_element_type=f32)

    def own_chip(side, owner):
        @pl.loop(0, 2)
        def _(half):
            at = pl.ds(pl.multiple_of(half * 256, 256), 256)
            got = product(t_hi[side, at, :], t_lo[side, at, :], hi[...], lo[...])
            aa[owner * 2 + half] = got.reshape(NZ, 16, COLS)

    keep = pl.multiple_of(low * HALF, HALF)

    def relay(e, q):
        piece = (pl.ds(q * TILE, TILE), pl.ds(e * 256, 256))
        arrived(cross.at[(0,) + piece], y_rs.at[e, q])
        send(cross.at[(0,) + piece], cross.at[(1,) + piece], relay_ss.at[e, q], relay_rs.at[e, q], twin)

    def turn_cross(side, e, q):
        rows = slice(q * TILE, (q + 1) * TILE)
        level = mean[pl.ds(keep + q * TILE, TILE), :]
        for j in (2 * e, 2 * e + 1):
            turn(cross[side, rows, j * TILE:(j + 1) * TILE] - level, q, c_hi.at[side], c_lo.at[side], j)

    def place(side, g, lane):
        index = side * 2 + lane // 2
        return 8 * g + (index + 2 if lane % 2 == g else (index + 6) % 8)

    def cross_chip(e):
        for q in range(HALF // TILE):
            turn_cross(0, e, q)
        for q in range(HALF // TILE):
            arrived(cross.at[1, pl.ds(q * TILE, TILE), pl.ds(e * 256, 256)], relay_rs.at[e, q])
            turn_cross(1, e, q)
        for side in range(2):
            for g in range(2):
                at = slice((2 * e + g) * TILE, (2 * e + g + 1) * TILE)
                got = product(c_hi[side, at, :], c_lo[side, at, :],
                              hi[pl.ds(keep, HALF), :], lo[pl.ds(keep, HALF), :])
                for j in range(4):
                    ab[e, place(side, g, j)] = got[:, j * TILE:(j + 1) * TILE]

    def z_step(t, part, slots_r, slots_l, ssr, rsr, ssl, rsl):
        to_r, to_l = (z + ZR - t + NZ) % NZ, (z + NZ - ZL + t) % NZ
        if 0 < t < ZR:
            arrived(slots_r.at[t - 1], rsr.at[t - 1])
            slots_r[t - 1] = slots_r[t - 1] + part[to_r]
        if t < ZR:
            src = part.at[to_r] if t == 0 else slots_r.at[t - 1]
            send(src, slots_r.at[t], ssr.at[t], rsr.at[t], zr)
        if 0 < t < ZL:
            arrived(slots_l.at[t - 1], rsl.at[t - 1])
            slots_l[t - 1] = slots_l[t - 1] + part[to_l]
        if t < ZL:
            src = part.at[to_l] if t == 0 else slots_l.at[t - 1]
            send(src, slots_l.at[t], ssl.at[t], rsl.at[t], zl)

    def z_last(part, slots_r, slots_l, rsr, rsl):
        arrived(slots_r.at[ZR - 1], rsr.at[ZR - 1])
        arrived(slots_l.at[ZL - 1], rsl.at[ZL - 1])
        return part[z] + slots_r[ZR - 1] + slots_l[ZL - 1]

    def unit_step(t):
        z_step(t, unit, unit_r, unit_l, ur_ss, ur_rs, ul_ss, ul_rs)

    def cross_step(e, t):
        z_step(t, ab.at[e], ab_r.at[e], ab_l.at[e], abr_ss.at[e], abr_rs.at[e], abl_ss.at[e], abl_rs.at[e])

    a_half, b_half = pl.ds(0, ZR), pl.ds(ZR, ZR)
    far, right, left = (x + 2) % NX, (x + 1) % NX, (x + NX - 1) % NX

    def x_first():
        send(aa.at[far, a_half], from_left.at[0], xr_ss.at[0], xr_rs.at[0], xr)
        send(aa.at[far, b_half], from_right.at[0], xl_ss.at[0], xl_rs.at[0], xl)
        send(aa.at[right, b_half], from_left.at[1], xr_ss.at[1], xr_rs.at[1], xr)
        send(aa.at[left, a_half], from_right.at[1], xl_ss.at[1], xl_rs.at[1], xl)

    def x_second():
        arrived(from_left.at[0], xr_rs.at[0])
        from_left[0] = from_left[0] + aa[right, a_half]
        send(from_left.at[0], from_left.at[2], xr_ss.at[2], xr_rs.at[2], xr)
        arrived(from_right.at[0], xl_rs.at[0])
        from_right[0] = from_right[0] + aa[left, b_half]
        send(from_right.at[0], from_right.at[2], xl_ss.at[2], xl_rs.at[2], xl)

    def x_last():
        for i in (1, 2):
            arrived(from_left.at[i], xr_rs.at[i])
            arrived(from_right.at[i], xl_rs.at[i])
        unit[a_half] = aa[x, a_half] + from_left[2] + from_right[1]
        unit[b_half] = aa[x, b_half] + from_left[1] + from_right[2]

    def e_over_x():
        e_x[3] = e_own[...] + jnp.sum(e_r[...], axis=0) + jnp.sum(e_l[...], axis=0)
        for i, target in enumerate((xr, xl, xx)):
            send(e_x.at[3], e_x.at[i], ex_ss.at[i], ex_rs.at[i], target)

    def e_over_h():
        for i in range(3):
            arrived(e_x.at[i], ex_rs.at[i])
        e_sum[...] = e_x[0] + e_x[1] + e_x[2] + e_x[3]
        send(e_sum, e_h, eh_ss, eh_rs, hh)

    def e_to_group():
        arrived(e_h, eh_rs)
        e_all[s] = e_sum[...] + e_h[...]
        for i, target in enumerate(group):
            send(e_all.at[s], e_all.at[s], eg_ss.at[i], eg_rs.at[i], target)

    def e_done():
        for i, d in enumerate((s ^ 1, s ^ 2, s ^ 3)):
            arrived(e_all.at[d], eg_rs.at[i])

    group8, spot = z // 8, z % 8
    index = (spot + 2) % 4
    middle = jnp.logical_and(spot >= 2, spot < 6)
    lane_tile = (index % 2) * 2 + jnp.where(middle, group8, 1 - group8)
    their = jnp.where(index // 2 == 0, core, 1 - core)
    me = x * NH + h

    def strip(e, k):
        ox, oz = 2 * (1 - low) + their, group8 * 8 + k
        own = jnp.logical_and(ox == x, jnp.logical_and(h == e, oz == z))
        return own, device(ox, e, oz, low, core)

    def cross_out(e):
        block = z_last(ab.at[e], ab_r.at[e], ab_l.at[e], abr_rs.at[e], abl_rs.at[e])
        flip[e, 0] = block
        flip[e, 1] = block.T

        @pl.loop(0, 8)
        def _(k):
            src = pl.ds(pl.multiple_of(k * 16, 16), 16)
            lanes = pl.ds(pl.multiple_of(lane_tile * TILE, TILE), TILE)
            own, owner = strip(e, k)

            wide = pl.ds(pl.multiple_of((2 * e + group8) * TILE, TILE), TILE)
            pltpu.make_async_remote_copy(
                src_ref=flip.at[e, 1, src], dst_ref=turned.at[me, :, wide],
                send_sem=fin_ss.at[9 + e * 16 + k], recv_sem=fin_rs.at[1],
                device_id=device(2 * low + core, lane_tile // 2, (lane_tile % 2) * 8 + k, 1 - low, their),
                device_id_type=MESH,
            ).start()

            @pl.when(own)
            def _():
                pltpu.make_async_copy(flip.at[e, 0, src], direct.at[me, :, lanes], fin_rs.at[0]).start()

            @pl.when(jnp.logical_not(own))
            def _():
                pltpu.make_async_remote_copy(
                    src_ref=flip.at[e, 0, src], dst_ref=direct.at[me, :, lanes],
                    send_sem=fin_ss.at[1 + e * 16 + k], recv_sem=fin_rs.at[0],
                    device_id=owner, device_id_type=MESH,
                ).start()

    own_chip(0, core)
    relay(0, 0)
    arrived(other, core_rs)
    for q in range(ROWS // TILE):
        rows = slice(q * TILE, (q + 1) * TILE)
        for j in range(4):
            turn(other[rows, j * TILE:(j + 1) * TILE] - mean[rows, :], q, t_hi.at[1], t_lo.at[1], j)
    relay(0, 1)
    own_chip(1, 1 - core)
    x_first()
    relay(0, 2)
    e_step(1)
    cross_chip(0)
    cross_step(0, 0)
    relay(1, 0)
    e_step(2)
    relay(1, 1)
    e_step(3)
    cross_step(0, 1)
    e_step(4)
    relay(1, 2)
    x_second()
    cross_step(0, 2)
    e_step(5)
    cross_chip(1)
    cross_step(1, 0)
    cross_step(0, 3)
    e_step(6)
    cross_step(1, 1)
    cross_step(0, 4)
    e_step(7)
    cross_step(1, 2)
    cross_step(0, 5)
    e_step(8)
    e_over_x()
    x_last()
    unit_step(0)
    cross_step(1, 3)
    cross_step(0, 6)
    unit_step(1)
    e_over_h()
    cross_step(1, 4)
    cross_step(0, 7)
    unit_step(2)
    e_to_group()
    cross_step(1, 5)
    unit_step(3)
    e_done()
    cross_out(0)
    cross_step(1, 6)
    unit_step(4)
    cross_step(1, 7)
    unit_step(5)
    cross_out(1)
    unit_step(6)
    unit_step(7)

    held[...] = z_last(unit, unit_r, unit_l, ur_rs, ul_rs)
    to_x, to_h = 2 * low + x // 2, x % 2
    mine = jnp.logical_and(to_x == x, to_h == h)

    @pl.when(mine)
    def _():
        pltpu.make_async_copy(held, direct.at[h], fin_rs.at[0]).start()

    @pl.when(jnp.logical_not(mine))
    def _():
        pltpu.make_async_remote_copy(
            src_ref=held, dst_ref=direct.at[h], send_sem=fin_ss.at[0], recv_sem=fin_rs.at[0],
            device_id=device(to_x, to_h, z, low, core), device_id_type=MESH,
        ).start()

    line = h * 2 + z // 8
    e_col[...] = jnp.broadcast_to(e_all[x, pl.ds(line, 1), :], (TILE, TILE)).T
    scale_j = lax.rsqrt(e_col[pl.ds(pl.multiple_of((z % 8) * 16, 16), 16), :] + eps)
    scale_i = lax.rsqrt(e_all[s] + eps)

    def finish(total):
        for j in range(4):
            lanes = slice(j * TILE, (j + 1) * TILE)
            out_ref[:, lanes] = total[:, lanes] * scale_i[j:j + 1, :] * scale_j

    @pl.when(x // 2 == low)
    def _():
        arrived(direct.at[pl.ds(0, 2)], fin_rs.at[0])
        finish(direct[0] + direct[1])

    @pl.when(x // 2 != low)
    def _():
        arrived(direct, fin_rs.at[0])
        arrived(turned, fin_rs.at[1])
        finish(jnp.sum(direct[...], axis=0) + jnp.sum(turned[...], axis=0))

    for src, sem in pending:
        arrived(src, sem)

    @pl.when(jnp.logical_not(mine))
    def _():
        arrived(held, fin_ss.at[0])

    for e in range(2):
        @pl.loop(0, 8)
        def _(k):
            src = flip.at[e, 0, pl.ds(0, 16)]
            own, _ = strip(e, k)

            @pl.when(jnp.logical_not(own))
            def _():
                arrived(src, fin_ss.at[1 + e * 16 + k])

            arrived(src, fin_ss.at[9 + e * 16 + k])


def per_device(snapshots):
    dma = pltpu.SemaphoreType.DMA
    vmem = pltpu.VMEM
    strip = pl.pallas_call(
        kernel,
        out_shape=jax.ShapeDtypeStruct((16, COLS), f32),
        in_specs=[pl.BlockSpec(memory_space=pltpu.VMEM)],
        out_specs=pl.BlockSpec(memory_space=pltpu.VMEM),
        scratch_shapes=[
            vmem((ROWS, COLS), f32),
            vmem((2, HALF, COLS), f32),
            vmem((4, 8, TILE), f32),
            vmem((ROWS, TILE), f32),
            vmem((ROWS, COLS), bf16), vmem((ROWS, COLS), bf16),
            vmem((2, COLS, ROWS), bf16), vmem((2, COLS, ROWS), bf16),
            vmem((2, COLS, HALF), bf16), vmem((2, COLS, HALF), bf16),
            vmem((4, NZ, 16, COLS), f32),
            vmem((2, NZ, TILE, TILE), f32),
            vmem((NZ, 16, COLS), f32),
            vmem((3, ZR, 16, COLS), f32), vmem((3, ZR, 16, COLS), f32),
            vmem((ZR, 16, COLS), f32), vmem((ZL, 16, COLS), f32),
            vmem((2, ZR, TILE, TILE), f32), vmem((2, ZL, TILE, TILE), f32),
            vmem((8, TILE), f32), vmem((ZR, 8, TILE), f32), vmem((ZL, 8, TILE), f32),
            vmem((4, 8, TILE), f32), vmem((8, TILE), f32), vmem((8, TILE), f32),
            vmem((4, 8, TILE), f32), vmem((TILE, TILE), f32),
            vmem((16, COLS), f32), vmem((2, 2, TILE, TILE), f32),
            vmem((8, 16, COLS), f32), vmem((8, 16, COLS), f32),
            dma, dma, dma((2, 3)), dma((2, 3)), dma((2, 3)), dma((2, 3)), dma((3,)), dma((3,)),
            dma((3,)), dma((3,)), dma((3,)), dma((3,)),
            dma((ZR,)), dma((ZR,)), dma((ZL,)), dma((ZL,)),
            dma((2, ZR)), dma((2, ZR)), dma((2, ZL)), dma((2, ZL)),
            dma((ZR,)), dma((ZR,)), dma((ZL,)), dma((ZL,)),
            dma((3,)), dma((3,)), dma, dma, dma((3,)), dma((3,)),
            dma((33,)), dma((2,)),
        ],
        compiler_params=pltpu.CompilerParams(
            collective_id=0, has_side_effects=True, vmem_limit_bytes=48 << 20
        ),
        cost_estimate=pl.CostEstimate(flops=3_600_000_000, bytes_accessed=1_700_000, transcendentals=0),
        name="gram",
    )(snapshots)
    return strip.T


def solution(mesh):
    return jax.shard_map(
        per_device, mesh=mesh, in_specs=(P("rows", "snap"),), out_specs=P("snap", "rows"), check_vma=False
    )
```

```python
import jax
import jax.numpy as jnp
from jax import lax
from jax.experimental import pallas as pl
from jax.experimental.pallas import tpu as pltpu
from jax.sharding import PartitionSpec as P

eps = 1e-06
MESH = pl.DeviceIdType.MESH
f32, bf16 = jnp.float32, jnp.bfloat16

NX, NH, NZ = 4, 2, 16
ROWS, COLS = 768, 512
HALF = ROWS // 2
TILE = 128
SNAPS = 2048
SUB = 2
WIDE = 4 // SUB
ZR, ZL = NZ // 2, NZ // 2 - 1


def device(x, h, z, low, core):
    return ((x * NH + h) * NZ + z, low * 2 + core)


def kernel(
    x_hbm, out_ref,
    x_ref, other, cross, sums, mean, hi, lo, t_hi, t_lo, c_hi, c_lo,
    aa, ab, unit, from_left, from_right,
    unit_re, unit_ro, unit_lo, unit_le, aa_r, aa_l,
    e_own, e_x, e_z, e_g, e_all, e_col,
    held, flip, direct, turned,
    in_sem, core_ss, core_rs, y_ss, y_rs, relay_ss, relay_rs, sum_ss, sum_rs,
    xr_ss, xr_rs, xl_ss, xl_rs,
    ure_ss, ure_rs, uro_ss, uro_rs, ulo_ss, ulo_rs, ule_ss, ule_rs, aar_ss, aar_rs, aal_ss, aal_rs,
    ex_ss, ex_rs, ez_ss, ez_rs, eg_ss, eg_rs,
    own_ss, fin_ss, fin_rs,
):
    r, s = lax.axis_index("rows"), lax.axis_index("snap")
    x, h, z = r // (NH * NZ), (r // NZ) % NH, r % NZ
    low, core = s // 2, s % 2
    zr, zl = device(x, h, (z + 1) % NZ, low, core), device(x, h, (z + NZ - 1) % NZ, low, core)
    zr2, zl2 = device(x, h, (z + 2) % NZ, low, core), device(x, h, (z + NZ - 2) % NZ, low, core)
    xr, xl = device((x + 1) % NX, h, z, low, core), device((x + NX - 1) % NX, h, z, low, core)
    xx = device((x + 2) % NX, h, z, low, core)
    hh = device(x, 1 - h, z, low, core)
    twin = device(x, h, z, low, 1 - core)
    pair = device(x, h, z, 1 - low, core)
    diagonal = device(x, h, z, 1 - low, 1 - core)
    group = (twin, pair, diagonal)
    pending = []

    def send(src, dst, send_sem, recv_sem, target):
        copy = pltpu.make_async_remote_copy(
            src_ref=src, dst_ref=dst, send_sem=send_sem, recv_sem=recv_sem,
            device_id=target, device_id_type=MESH,
        )
        copy.start()
        pending.append((src, send_sem))
        return copy

    def arrived(dst, sem):
        pltpu.make_async_copy(dst, dst, sem).wait()

    def load(q):
        rows = pl.ds(q * TILE, TILE)
        return pltpu.make_async_copy(x_hbm.at[rows], x_ref.at[rows], in_sem.at[q])

    for q in range(ROWS // TILE):
        load(q).start()
    barrier = pltpu.get_barrier_semaphore()
    near = (twin, pair, diagonal, zr, zl, zr2, zl2, xr, xl, xx, hh)
    for target in near:
        pl.semaphore_signal(barrier, inc=1, device_id=target, device_id_type=MESH)

    def row_sums(q):
        load(q).wait()
        block = x_ref[q * TILE:(q + 1) * TILE, :]
        part = block[:, 0:128] + block[:, 128:256] + block[:, 256:384] + block[:, 384:512]
        sums[s, q:q + 1, :] = jnp.sum(part.T, axis=0, keepdims=True)

    for q in range(ROWS // TILE):
        row_sums(q)
    sums[s, 6:8, :] = jnp.zeros((2, TILE), f32)
    pl.semaphore_wait(barrier, len(near))

    for i, target in enumerate(group):
        send(sums.at[s], sums.at[s], sum_ss.at[i], sum_rs.at[i], target)
    give = pl.multiple_of((1 - low) * HALF, HALF)
    for e in range(2):
        for q in range(HALF // TILE):
            lanes = pl.ds(e * 256, 256)
            send(x_ref.at[pl.ds(give + q * TILE, TILE), lanes], cross.at[0, pl.ds(q * TILE, TILE), lanes],
                 y_ss.at[e, q], y_rs.at[e, q], pair)
        if e == 0:
            send(x_ref, other, core_ss, core_rs, twin)

    for i, d in enumerate((s ^ 1, s ^ 2, s ^ 3)):
        arrived(sums.at[d], sum_rs.at[i])
    mean_rows = (sums[0] + sums[1] + sums[2] + sums[3]) / SNAPS
    for q in range(ROWS // TILE):
        wide = jnp.broadcast_to(mean_rows[q:q + 1, :], (TILE, TILE))
        mean[q * TILE:(q + 1) * TILE, :] = wide.T

    def split(value):
        high = value.astype(bf16)
        return high, (value - high.astype(f32)).astype(bf16)

    def turn(block, q, to_hi, to_lo, j):
        high, rest = split(block.T)
        to_hi[j * TILE:(j + 1) * TILE, q * TILE:(q + 1) * TILE] = high
        to_lo[j * TILE:(j + 1) * TILE, q * TILE:(q + 1) * TILE] = rest

    energy = [jnp.zeros((8, TILE), f32) for _ in range(4)]
    for q in range(ROWS // TILE):
        rows = slice(q * TILE, (q + 1) * TILE)
        for j in range(4):
            block = x_ref[rows, j * TILE:(j + 1) * TILE] - mean[rows, :]
            energy[j] += jnp.sum((block * block).reshape(TILE // 8, 8, TILE), axis=0)
            high, rest = split(block)
            hi[rows, j * TILE:(j + 1) * TILE] = high
            lo[rows, j * TILE:(j + 1) * TILE] = rest
            turn(block, q, t_hi.at[0], t_lo.at[0], j)
    for j in range(4):
        e_own[j:j + 1, :] = jnp.sum(energy[j], axis=0, keepdims=True)
    e_own[4:8, :] = jnp.zeros((4, TILE), f32)

    z1 = device(x, h, z + 1 - 2 * (z % 2), low, core)
    z2 = device(x, h, z + 2 - 4 * ((z // 2) % 2), low, core)
    z4r, z4l = device(x, h, (z + 4) % NZ, low, core), device(x, h, (z + NZ - 4) % NZ, low, core)

    def e_step(t):
        if t == 0:
            for i, target in enumerate((xr, xl, xx)):
                send(e_own, e_x.at[i], ex_ss.at[i], ex_rs.at[i], target)
        elif t == 1:
            for i in range(3):
                arrived(e_x.at[i], ex_rs.at[i])
            e_z[0] = e_own[...] + e_x[0] + e_x[1] + e_x[2]
            send(e_z.at[0], e_g.at[0], ez_ss.at[0], ez_rs.at[0], hh)
        elif t in (2, 3, 4):
            arrived(e_g.at[t - 2], ez_rs.at[t - 2])
            e_z[t - 1] = e_z[t - 2] + e_g[t - 2]
            if t < 4:
                send(e_z.at[t - 1], e_g.at[t - 1], ez_ss.at[t - 1], ez_rs.at[t - 1], z1 if t == 2 else z2)
            else:
                send(e_z.at[3], e_g.at[3], ez_ss.at[3], ez_rs.at[3], z4r)
                send(e_z.at[3], e_g.at[4], ez_ss.at[4], ez_rs.at[4], z4l)
        elif t == 5:
            arrived(e_g.at[3], ez_rs.at[3])
            send(e_g.at[3], e_g.at[5], ez_ss.at[5], ez_rs.at[5], z4r)
            arrived(e_g.at[4], ez_rs.at[4])
        elif t == 6:
            arrived(e_g.at[5], ez_rs.at[5])
            e_all[s] = e_z[3] + e_g[3] + e_g[4] + e_g[5]
            for i, target in enumerate(group):
                send(e_all.at[s], e_all.at[s], eg_ss.at[i], eg_rs.at[i], target)
        else:
            for i, d in enumerate((s ^ 1, s ^ 2, s ^ 3)):
                arrived(e_all.at[d], eg_rs.at[i])

    e_step(0)

    def product(a_hi, a_lo, b_hi, b_lo):
        total = jnp.dot(a_hi, b_hi, preferred_element_type=f32)
        total += jnp.dot(a_hi, b_lo, preferred_element_type=f32)
        return total + jnp.dot(a_lo, b_hi, preferred_element_type=f32)

    def own_chip(side):
        got = product(t_hi[side], t_lo[side], hi[...], lo[...])
        for half in range(2):
            aa[:, side * 2 + half] = got[half * 256:(half + 1) * 256].reshape(NZ, 16, COLS)

    keep = pl.multiple_of(low * HALF, HALF)

    def relay(e, q):
        piece = (pl.ds(q * TILE, TILE), pl.ds(e * 256, 256))
        arrived(cross.at[(0,) + piece], y_rs.at[e, q])
        send(cross.at[(0,) + piece], cross.at[(1,) + piece], relay_ss.at[e, q], relay_rs.at[e, q], twin)

    def turn_cross(side, e, q):
        if side == 1:
            arrived(cross.at[1, pl.ds(q * TILE, TILE), pl.ds(e * 256, 256)], relay_rs.at[e, q])
        rows = slice(q * TILE, (q + 1) * TILE)
        level = mean[pl.ds(keep + q * TILE, TILE), :]
        for g in range(2):
            lanes = slice((2 * e + g) * TILE, (2 * e + g + 1) * TILE)
            turn(cross[side, rows, lanes] - level, q, c_hi.at[e], c_lo.at[e], side * 2 + g)

    def cross_chip(e):
        got = product(c_hi[e], c_lo[e], hi[pl.ds(keep, HALF), :], lo[pl.ds(keep, HALF), :])
        for side in range(2):
            for g in range(2):
                for j in range(4):
                    for k in range(4):
                        at = (side * 2 + g) * TILE + k * 32
                        ab[e, j, 8 * g + 2 * k + side] = got[at:at + 32, j * TILE:(j + 1) * TILE]

    def hop(t, part, slots, ss, rs, target):
        src = part if t == 0 else slots.at[t - 1]
        if t > 0:
            arrived(slots.at[t - 1], rs.at[t - 1])
            slots[t - 1] = slots[t - 1] + part[...]
        send(src, slots.at[t], ss.at[t], rs.at[t], target)

    def unit_step(e, t):
        def one(distance, slots, ss, rs, target):
            hop(t, unit.at[e, (z + distance) % NZ], slots.at[e], ss.at[e], rs.at[e], target)

        one(8 - 2 * t, unit_re, ure_ss, ure_rs, zr2)
        one(9 + 2 * t, unit_lo, ulo_ss, ulo_rs, zl2 if t < 3 else zl)
        one(7 - 2 * t, unit_ro, uro_ss, uro_rs, zr2 if t < 3 else zr)
        if t < 3:
            one(10 + 2 * t, unit_le, ule_ss, ule_rs, zl2)

    def unit_last(e):
        total = unit[e, z]
        for slots, rs, n in ((unit_le, ule_rs, 3), (unit_re, ure_rs, 4), (unit_ro, uro_rs, 4), (unit_lo, ulo_rs, 4)):
            arrived(slots.at[e, n - 1], rs.at[e, n - 1])
            total = total + slots[e, n - 1]
        return total

    def own_step(u, t):
        half = pl.ds(WIDE * u, WIDE)
        if t < ZR:
            hop(t, aa.at[(z + ZR - t) % NZ, half], aa_r.at[u], aar_ss.at[u], aar_rs.at[u], zr)
        if t < ZL:
            hop(t, aa.at[(z + NZ - ZL + t) % NZ, half], aa_l.at[u], aal_ss.at[u], aal_rs.at[u], zl)

    def own_owner(u):
        ox, oh = 2 * low + (core if u < 2 else 1 - core), u % 2
        return jnp.logical_and(ox == x, oh == h), device(ox, oh, z, low, core)

    def own_out():
        for u in range(SUB):
            arrived(aa_r.at[u, ZR - 1], aar_rs.at[u, ZR - 1])
            arrived(aa_l.at[u, ZL - 1], aal_rs.at[u, ZL - 1])
            half = pl.ds(WIDE * u, WIDE)
            held[half] = aa[z, half] + aa_r[u, ZR - 1] + aa_l[u, ZL - 1]
        for u in range(4):
            mine, owner = own_owner(u)

            @pl.when(mine)
            def _():
                pltpu.make_async_copy(held.at[u], direct.at[me], fin_rs.at[0]).start()

            @pl.when(jnp.logical_not(mine))
            def _():
                pltpu.make_async_remote_copy(
                    src_ref=held.at[u], dst_ref=direct.at[me], send_sem=own_ss.at[u], recv_sem=fin_rs.at[0],
                    device_id=owner, device_id_type=MESH,
                ).start()

    a_half, b_half = pl.ds(0, ZR), pl.ds(ZR, ZR)
    far, right, left = (x + 2) % NX, (x + 1) % NX, (x + NX - 1) % NX

    def x_first(e):
        part, by_l, by_r = ab.at[e], from_left.at[e], from_right.at[e]
        send(part.at[far, a_half], by_l.at[0], xr_ss.at[e, 0], xr_rs.at[e, 0], xr)
        send(part.at[far, b_half], by_r.at[0], xl_ss.at[e, 0], xl_rs.at[e, 0], xl)
        send(part.at[right, b_half], by_l.at[1], xr_ss.at[e, 1], xr_rs.at[e, 1], xr)
        send(part.at[left, a_half], by_r.at[1], xl_ss.at[e, 1], xl_rs.at[e, 1], xl)

    def x_second(e):
        part, by_l, by_r = ab.at[e], from_left.at[e], from_right.at[e]
        arrived(by_l.at[0], xr_rs.at[e, 0])
        by_l[0] = by_l[0] + part[right, a_half]
        send(by_l.at[0], by_l.at[2], xr_ss.at[e, 2], xr_rs.at[e, 2], xr)
        arrived(by_r.at[0], xl_rs.at[e, 0])
        by_r[0] = by_r[0] + part[left, b_half]
        send(by_r.at[0], by_r.at[2], xl_ss.at[e, 2], xl_rs.at[e, 2], xl)

    def x_last(e):
        for i in (1, 2):
            arrived(from_left.at[e, i], xr_rs.at[e, i])
            arrived(from_right.at[e, i], xl_rs.at[e, i])
        unit[e, a_half] = ab[e, x, a_half] + from_left[e, 2] + from_right[e, 1]
        unit[e, b_half] = ab[e, x, b_half] + from_left[e, 1] + from_right[e, 2]

    group8, quarter = z // 8, (z % 8) // 2
    their = jnp.where(z % 2 == 0, core, 1 - core)
    me = x * NH + h

    def strip(e, k):
        ox, oz = 2 * (1 - low) + their, group8 * 8 + quarter * 2 + k
        own = jnp.logical_and(ox == x, jnp.logical_and(h == e, oz == z))
        return own, device(ox, e, oz, low, core)

    def cross_out(e):
        block = unit_last(e)
        flip[e, 0, 0:32, :] = block
        column = lax.broadcasted_iota(jnp.int32, (TILE, TILE), 1)
        tall = jnp.concatenate([block] * 4, axis=0).T
        flip[e, 1] = jnp.where(column // 32 == quarter, tall, 0.0)
        wide = pl.ds(pl.multiple_of((2 * e + group8) * TILE, TILE), TILE)
        lanes = pl.ds(pl.multiple_of(x * TILE, TILE), TILE)

        @pl.loop(0, 8)
        def _(k):
            src = pl.ds(pl.multiple_of(k * 16, 16), 16)
            pltpu.make_async_remote_copy(
                src_ref=flip.at[e, 1, src], dst_ref=turned.at[quarter * 2 + h, :, wide],
                send_sem=fin_ss.at[e, 2 + k], recv_sem=fin_rs.at[1],
                device_id=device(2 * low + core, x // 2, (x % 2) * 8 + k, 1 - low, their),
                device_id_type=MESH,
            ).start()

        for k in range(2):
            src = pl.ds(k * 16, 16)
            own, owner = strip(e, k)

            @pl.when(own)
            def _():
                pltpu.make_async_copy(flip.at[e, 0, src], direct.at[h, :, lanes], fin_rs.at[0]).start()

            @pl.when(jnp.logical_not(own))
            def _():
                pltpu.make_async_remote_copy(
                    src_ref=flip.at[e, 0, src], dst_ref=direct.at[h, :, lanes],
                    send_sem=fin_ss.at[e, k], recv_sem=fin_rs.at[0],
                    device_id=owner, device_id_type=MESH,
                ).start()

    def other_chip():
        arrived(other, core_rs)
        for q in range(ROWS // TILE):
            rows = slice(q * TILE, (q + 1) * TILE)
            for j in range(4):
                turn(other[rows, j * TILE:(j + 1) * TILE] - mean[rows, :], q, t_hi.at[1], t_lo.at[1], j)

    own_chip(0)
    relay(0, 0)
    other_chip()
    relay(0, 1)
    own_chip(1)
    for u in range(SUB): own_step(u, 0)
    relay(0, 2)
    turn_cross(0, 0, 0)
    turn_cross(0, 0, 1)
    turn_cross(0, 0, 2)
    turn_cross(1, 0, 0)
    turn_cross(1, 0, 1)
    turn_cross(1, 0, 2)
    e_step(1)
    cross_chip(0)
    x_first(0)
    for u in range(SUB): own_step(u, 1)
    relay(1, 0)
    turn_cross(0, 1, 0)
    e_step(2)
    relay(1, 1)
    turn_cross(0, 1, 1)
    turn_cross(1, 1, 0)
    turn_cross(1, 1, 1)
    for u in range(SUB): own_step(u, 2)
    x_second(0)
    relay(1, 2)
    turn_cross(0, 1, 2)
    turn_cross(1, 1, 2)
    e_step(3)
    cross_chip(1)
    x_first(1)
    for u in range(SUB): own_step(u, 3)
    x_last(0)
    unit_step(0, 0)
    x_second(1)
    for u in range(SUB): own_step(u, 4)
    unit_step(0, 1)
    e_step(4)
    for u in range(SUB): own_step(u, 5)
    unit_step(0, 2)
    x_last(1)
    unit_step(1, 0)
    e_step(5)
    for u in range(SUB): own_step(u, 6)
    unit_step(0, 3)
    unit_step(1, 1)
    e_step(6)
    for u in range(SUB): own_step(u, 7)
    e_step(7)
    cross_out(0)
    unit_step(1, 2)
    own_out()
    unit_step(1, 3)
    cross_out(1)

    line = h * 2 + z // 8
    e_col[...] = jnp.broadcast_to(e_all[x, pl.ds(line, 1), :], (TILE, TILE)).T
    scale_j = lax.rsqrt(e_col[pl.ds(pl.multiple_of((z % 8) * 16, 16), 16), :] + eps)
    scale_i = lax.rsqrt(e_all[s] + eps)

    def finish(total):
        for j in range(4):
            lanes = slice(j * TILE, (j + 1) * TILE)
            out_ref[:, lanes] = total[:, lanes] * scale_i[j:j + 1, :] * scale_j

    for src, sem in pending:
        arrived(src, sem)

    @pl.when(x // 2 == low)
    def _():
        arrived(direct, fin_rs.at[0])
        finish(jnp.sum(direct[...], axis=0))

    @pl.when(x // 2 != low)
    def _():
        arrived(direct.at[pl.ds(0, 2)], fin_rs.at[0])
        arrived(turned, fin_rs.at[1])
        finish(direct[0] + direct[1] + jnp.sum(turned[...], axis=0))

    for u in range(4):
        mine, _ = own_owner(u)

        @pl.when(jnp.logical_not(mine))
        def _():
            arrived(held.at[u], own_ss.at[u])

    for e in range(2):
        src = flip.at[e, 0, pl.ds(0, 16)]
        for k in range(2):
            own, _ = strip(e, k)

            @pl.when(jnp.logical_not(own))
            def _():
                arrived(src, fin_ss.at[e, k])

        @pl.loop(0, 8)
        def _(k):
            arrived(src, fin_ss.at[e, 2 + k])


def per_device(snapshots):
    dma = pltpu.SemaphoreType.DMA
    vmem = pltpu.VMEM
    strip = pl.pallas_call(
        kernel,
        out_shape=jax.ShapeDtypeStruct((16, COLS), f32),
        in_specs=[pl.BlockSpec(memory_space=pl.ANY)],
        out_specs=pl.BlockSpec(memory_space=pltpu.VMEM),
        scratch_shapes=[
            vmem((ROWS, COLS), f32), vmem((ROWS, COLS), f32),
            vmem((2, HALF, COLS), f32),
            vmem((4, 8, TILE), f32),
            vmem((ROWS, TILE), f32),
            vmem((ROWS, COLS), bf16), vmem((ROWS, COLS), bf16),
            vmem((2, COLS, ROWS), bf16), vmem((2, COLS, ROWS), bf16),
            vmem((2, COLS, HALF), bf16), vmem((2, COLS, HALF), bf16),
            vmem((NZ, 4, 16, COLS), f32),
            vmem((2, NX, NZ, 32, TILE), f32),
            vmem((2, NZ, 32, TILE), f32),
            vmem((2, 3, ZR, 32, TILE), f32), vmem((2, 3, ZR, 32, TILE), f32),
            vmem((2, 4, 32, TILE), f32), vmem((2, 4, 32, TILE), f32),
            vmem((2, 4, 32, TILE), f32), vmem((2, 3, 32, TILE), f32),
            vmem((SUB, ZR, WIDE, 16, COLS), f32), vmem((SUB, ZL, WIDE, 16, COLS), f32),
            vmem((8, TILE), f32), vmem((3, 8, TILE), f32),
            vmem((4, 8, TILE), f32), vmem((6, 8, TILE), f32),
            vmem((4, 8, TILE), f32), vmem((TILE, TILE), f32),
            vmem((4, 16, COLS), f32), vmem((2, 2, TILE, TILE), f32),
            vmem((8, 16, COLS), f32), vmem((8, 16, COLS), f32),
            dma((6,)), dma, dma, dma((2, 3)), dma((2, 3)), dma((2, 3)), dma((2, 3)), dma((3,)), dma((3,)),
            dma((2, 3)), dma((2, 3)), dma((2, 3)), dma((2, 3)),
            dma((2, 4)), dma((2, 4)), dma((2, 4)), dma((2, 4)), dma((2, 4)), dma((2, 4)), dma((2, 3)), dma((2, 3)),
            dma((SUB, ZR)), dma((SUB, ZR)), dma((SUB, ZL)), dma((SUB, ZL)),
            dma((3,)), dma((3,)), dma((6,)), dma((6,)), dma((3,)), dma((3,)),
            dma((4,)), dma((2, 10)), dma((2,)),
        ],
        compiler_params=pltpu.CompilerParams(
            collective_id=0, has_side_effects=True, vmem_limit_bytes=48 << 20
        ),
        cost_estimate=pl.CostEstimate(flops=3_600_000_000, bytes_accessed=1_700_000, transcendentals=0),
        name="gram",
    )(snapshots)
    return strip.T


def solution(mesh):
    return jax.shard_map(
        per_device, mesh=mesh, in_specs=(P("rows", "snap"),), out_specs=P("snap", "rows"), check_vma=False
    )
```

```python
import jax
import jax.numpy as jnp
from jax import lax
from jax.experimental import pallas as pl
from jax.experimental.pallas import tpu as pltpu
from jax.sharding import PartitionSpec as P

eps = 1e-06
MESH = pl.DeviceIdType.MESH
f32, bf16 = jnp.float32, jnp.bfloat16

NX, NH, NZ = 4, 2, 16
ROWS, COLS = 768, 512
HALF = ROWS // 2
TILE = 128
SNAPS = 2048
SUB = 2
WIDE = 4 // SUB
ZR, ZL = NZ // 2, NZ // 2 - 1


def device(x, h, z, low, core):
    return ((x * NH + h) * NZ + z, low * 2 + core)


def kernel(
    x_hbm, out_ref,
    x_ref, other, cross, sums, mean, hi, lo, t_hi, t_lo, c_hi, c_lo,
    aa, ab, unit, from_left, from_right,
    unit_re, unit_ro, unit_lo, unit_le, aa_r, aa_l,
    e_own, e_x, e_z, e_g, e_all, e_col,
    held, flip, direct, turned,
    in_sem, core_ss, core_rs, y_ss, y_rs, relay_ss, relay_rs, sum_ss, sum_rs,
    xr_ss, xr_rs, xl_ss, xl_rs,
    ure_ss, ure_rs, uro_ss, uro_rs, ulo_ss, ulo_rs, ule_ss, ule_rs, aar_ss, aar_rs, aal_ss, aal_rs,
    ex_ss, ex_rs, ez_ss, ez_rs, eg_ss, eg_rs,
    own_ss, fin_ss, fin_rs,
):
    r, s = lax.axis_index("rows"), lax.axis_index("snap")
    x, h, z = r // (NH * NZ), (r // NZ) % NH, r % NZ
    low, core = s // 2, s % 2
    zr, zl = device(x, h, (z + 1) % NZ, low, core), device(x, h, (z + NZ - 1) % NZ, low, core)
    zr2, zl2 = device(x, h, (z + 2) % NZ, low, core), device(x, h, (z + NZ - 2) % NZ, low, core)
    xr, xl = device((x + 1) % NX, h, z, low, core), device((x + NX - 1) % NX, h, z, low, core)
    xx = device((x + 2) % NX, h, z, low, core)
    hh = device(x, 1 - h, z, low, core)
    twin = device(x, h, z, low, 1 - core)
    pair = device(x, h, z, 1 - low, core)
    diagonal = device(x, h, z, 1 - low, 1 - core)
    group = (twin, pair, diagonal)
    pending = []

    def send(src, dst, send_sem, recv_sem, target):
        copy = pltpu.make_async_remote_copy(
            src_ref=src, dst_ref=dst, send_sem=send_sem, recv_sem=recv_sem,
            device_id=target, device_id_type=MESH,
        )
        copy.start()
        pending.append((src, send_sem))
        return copy

    def arrived(dst, sem):
        pltpu.make_async_copy(dst, dst, sem).wait()

    def load(q):
        rows = pl.ds(q * TILE, TILE)
        return pltpu.make_async_copy(x_hbm.at[rows], x_ref.at[rows], in_sem.at[q])

    for q in range(ROWS // TILE):
        load(q).start()
    barrier = pltpu.get_barrier_semaphore()
    near = (twin, pair, diagonal, zr, zl, zr2, zl2, xr, xl, xx, hh)
    for target in near:
        pl.semaphore_signal(barrier, inc=1, device_id=target, device_id_type=MESH)

    def row_sums(q):
        load(q).wait()
        block = x_ref[q * TILE:(q + 1) * TILE, :]
        part = block[:, 0:128] + block[:, 128:256] + block[:, 256:384] + block[:, 384:512]
        sums[s, q:q + 1, :] = jnp.sum(part.T, axis=0, keepdims=True)

    for q in range(ROWS // TILE):
        row_sums(q)
    sums[s, 6:8, :] = jnp.zeros((2, TILE), f32)
    pl.semaphore_wait(barrier, len(near))

    for i, target in enumerate(group):
        send(sums.at[s], sums.at[s], sum_ss.at[i], sum_rs.at[i], target)
    give = pl.multiple_of((1 - low) * HALF, HALF)
    for e in range(2):
        for q in range(HALF // TILE):
            lanes = pl.ds(e * 256, 256)
            send(x_ref.at[pl.ds(give + q * TILE, TILE), lanes], cross.at[0, pl.ds(q * TILE, TILE), lanes],
                 y_ss.at[e, q], y_rs.at[e, q], pair)
        if e == 0:
            send(x_ref, other, core_ss, core_rs, twin)

    for i, d in enumerate((s ^ 1, s ^ 2, s ^ 3)):
        arrived(sums.at[d], sum_rs.at[i])
    mean_rows = (sums[0] + sums[1] + sums[2] + sums[3]) / SNAPS
    for q in range(ROWS // TILE):
        wide = jnp.broadcast_to(mean_rows[q:q + 1, :], (TILE, TILE))
        mean[q * TILE:(q + 1) * TILE, :] = wide.T

    def split(value):
        high = value.astype(bf16)
        return high, (value - high.astype(f32)).astype(bf16)

    def turn(block, q, to_hi, to_lo, j):
        high, rest = split(block.T)
        to_hi[j * TILE:(j + 1) * TILE, q * TILE:(q + 1) * TILE] = high
        to_lo[j * TILE:(j + 1) * TILE, q * TILE:(q + 1) * TILE] = rest

    energy = [jnp.zeros((8, TILE), f32) for _ in range(4)]
    for q in range(ROWS // TILE):
        rows = slice(q * TILE, (q + 1) * TILE)
        for j in range(4):
            block = x_ref[rows, j * TILE:(j + 1) * TILE] - mean[rows, :]
            energy[j] += jnp.sum((block * block).reshape(TILE // 8, 8, TILE), axis=0)
            high, rest = split(block)
            hi[rows, j * TILE:(j + 1) * TILE] = high
            lo[rows, j * TILE:(j + 1) * TILE] = rest
            turn(block, q, t_hi.at[0], t_lo.at[0], j)
    for j in range(4):
        e_own[j:j + 1, :] = jnp.sum(energy[j], axis=0, keepdims=True)
    e_own[4:8, :] = jnp.zeros((4, TILE), f32)

    z1 = device(x, h, z + 1 - 2 * (z % 2), low, core)
    z2 = device(x, h, z + 2 - 4 * ((z // 2) % 2), low, core)
    z4r, z4l = device(x, h, (z + 4) % NZ, low, core), device(x, h, (z + NZ - 4) % NZ, low, core)

    def e_step(t):
        if t == 0:
            send(e_own, e_g.at[0], ez_ss.at[0], ez_rs.at[0], z1)
        elif t == 1:
            arrived(e_g.at[0], ez_rs.at[0])
            e_z[0] = e_own[...] + e_g[0]
            send(e_z.at[0], e_g.at[1], ez_ss.at[1], ez_rs.at[1], z2)
        elif t == 2:
            arrived(e_g.at[1], ez_rs.at[1])
            e_z[1] = e_z[0] + e_g[1]
            for i, target in enumerate((xr, xl, xx)):
                send(e_z.at[1], e_x.at[i], ex_ss.at[i], ex_rs.at[i], target)
        elif t == 3:
            for i in range(3):
                arrived(e_x.at[i], ex_rs.at[i])
            e_z[2] = e_z[1] + e_x[0] + e_x[1] + e_x[2]
            send(e_z.at[2], e_g.at[2], ez_ss.at[2], ez_rs.at[2], hh)
        elif t == 4:
            arrived(e_g.at[2], ez_rs.at[2])
            e_z[3] = e_z[2] + e_g[2]
            send(e_z.at[3], e_g.at[3], ez_ss.at[3], ez_rs.at[3], z4r)
            send(e_z.at[3], e_g.at[4], ez_ss.at[4], ez_rs.at[4], z4l)
        elif t == 5:
            arrived(e_g.at[3], ez_rs.at[3])
            send(e_g.at[3], e_g.at[5], ez_ss.at[5], ez_rs.at[5], z4r)
            arrived(e_g.at[4], ez_rs.at[4])
        elif t == 6:
            arrived(e_g.at[5], ez_rs.at[5])
            e_all[s] = e_z[3] + e_g[3] + e_g[4] + e_g[5]
            for i, target in enumerate(group):
                send(e_all.at[s], e_all.at[s], eg_ss.at[i], eg_rs.at[i], target)
        else:
            for i, d in enumerate((s ^ 1, s ^ 2, s ^ 3)):
                arrived(e_all.at[d], eg_rs.at[i])

    e_step(0)

    def product(a_hi, a_lo, b_hi, b_lo):
        total = jnp.dot(a_hi, b_hi, preferred_element_type=f32)
        total += jnp.dot(a_hi, b_lo, preferred_element_type=f32)
        return total + jnp.dot(a_lo, b_hi, preferred_element_type=f32)

    def own_chip(side):
        got = product(t_hi[side], t_lo[side], hi[...], lo[...])
        for half in range(2):
            aa[:, side * 2 + half] = got[half * 256:(half + 1) * 256].reshape(NZ, 16, COLS)

    keep = pl.multiple_of(low * HALF, HALF)

    def relay(e, q):
        piece = (pl.ds(q * TILE, TILE), pl.ds(e * 256, 256))
        arrived(cross.at[(0,) + piece], y_rs.at[e, q])
        send(cross.at[(0,) + piece], cross.at[(1,) + piece], relay_ss.at[e, q], relay_rs.at[e, q], twin)

    def turn_cross(side, e, q):
        if side == 1:
            arrived(cross.at[1, pl.ds(q * TILE, TILE), pl.ds(e * 256, 256)], relay_rs.at[e, q])
        rows = slice(q * TILE, (q + 1) * TILE)
        level = mean[pl.ds(keep + q * TILE, TILE), :]
        for g in range(2):
            lanes = slice((2 * e + g) * TILE, (2 * e + g + 1) * TILE)
            turn(cross[side, rows, lanes] - level, q, c_hi.at[e], c_lo.at[e], side * 2 + g)

    def cross_chip(e):
        got = product(c_hi[e], c_lo[e], hi[pl.ds(keep, HALF), :], lo[pl.ds(keep, HALF), :])
        for side in range(2):
            for g in range(2):
                for j in range(4):
                    for k in range(4):
                        at = (side * 2 + g) * TILE + k * 32
                        ab[e, j, 8 * g + 2 * k + side] = got[at:at + 32, j * TILE:(j + 1) * TILE]

    def hop(t, part, slots, ss, rs, target):
        src = part if t == 0 else slots.at[t - 1]
        if t > 0:
            arrived(slots.at[t - 1], rs.at[t - 1])
            slots[t - 1] = slots[t - 1] + part[...]
        send(src, slots.at[t], ss.at[t], rs.at[t], target)

    def unit_step(e, t):
        def one(distance, slots, ss, rs, target):
            hop(t, unit.at[e, (z + distance) % NZ], slots.at[e], ss.at[e], rs.at[e], target)

        one(8 - 2 * t, unit_re, ure_ss, ure_rs, zr2)
        one(9 + 2 * t, unit_lo, ulo_ss, ulo_rs, zl2 if t < 3 else zl)
        one(7 - 2 * t, unit_ro, uro_ss, uro_rs, zr2 if t < 3 else zr)
        if t < 3:
            one(10 + 2 * t, unit_le, ule_ss, ule_rs, zl2)

    def unit_last(e):
        total = unit[e, z]
        for slots, rs, n in ((unit_le, ule_rs, 3), (unit_re, ure_rs, 4), (unit_ro, uro_rs, 4), (unit_lo, ulo_rs, 4)):
            arrived(slots.at[e, n - 1], rs.at[e, n - 1])
            total = total + slots[e, n - 1]
        return total

    def own_step(u, t):
        half = pl.ds(WIDE * u, WIDE)
        if t < ZR:
            hop(t, aa.at[(z + ZR - t) % NZ, half], aa_r.at[u], aar_ss.at[u], aar_rs.at[u], zr)
        if t < ZL:
            hop(t, aa.at[(z + NZ - ZL + t) % NZ, half], aa_l.at[u], aal_ss.at[u], aal_rs.at[u], zl)

    def own_owner(u):
        ox, oh = 2 * low + (core if u < 2 else 1 - core), u % 2
        return jnp.logical_and(ox == x, oh == h), device(ox, oh, z, low, core)

    def own_out():
        for u in range(SUB):
            arrived(aa_r.at[u, ZR - 1], aar_rs.at[u, ZR - 1])
            arrived(aa_l.at[u, ZL - 1], aal_rs.at[u, ZL - 1])
            half = pl.ds(WIDE * u, WIDE)
            held[half] = aa[z, half] + aa_r[u, ZR - 1] + aa_l[u, ZL - 1]
        for u in range(4):
            mine, owner = own_owner(u)

            @pl.when(mine)
            def _():
                pltpu.make_async_copy(held.at[u], direct.at[me], fin_rs.at[0]).start()

            @pl.when(jnp.logical_not(mine))
            def _():
                pltpu.make_async_remote_copy(
                    src_ref=held.at[u], dst_ref=direct.at[me], send_sem=own_ss.at[u], recv_sem=fin_rs.at[0],
                    device_id=owner, device_id_type=MESH,
                ).start()

    a_half, b_half = pl.ds(0, ZR), pl.ds(ZR, ZR)
    far, right, left = (x + 2) % NX, (x + 1) % NX, (x + NX - 1) % NX

    def x_first(e):
        part, by_l, by_r = ab.at[e], from_left.at[e], from_right.at[e]
        send(part.at[far, a_half], by_l.at[0], xr_ss.at[e, 0], xr_rs.at[e, 0], xr)
        send(part.at[far, b_half], by_r.at[0], xl_ss.at[e, 0], xl_rs.at[e, 0], xl)
        send(part.at[right, b_half], by_l.at[1], xr_ss.at[e, 1], xr_rs.at[e, 1], xr)
        send(part.at[left, a_half], by_r.at[1], xl_ss.at[e, 1], xl_rs.at[e, 1], xl)

    def x_second(e):
        part, by_l, by_r = ab.at[e], from_left.at[e], from_right.at[e]
        arrived(by_l.at[0], xr_rs.at[e, 0])
        by_l[0] = by_l[0] + part[right, a_half]
        send(by_l.at[0], by_l.at[2], xr_ss.at[e, 2], xr_rs.at[e, 2], xr)
        arrived(by_r.at[0], xl_rs.at[e, 0])
        by_r[0] = by_r[0] + part[left, b_half]
        send(by_r.at[0], by_r.at[2], xl_ss.at[e, 2], xl_rs.at[e, 2], xl)

    def x_last(e):
        for i in (1, 2):
            arrived(from_left.at[e, i], xr_rs.at[e, i])
            arrived(from_right.at[e, i], xl_rs.at[e, i])
        unit[e, a_half] = ab[e, x, a_half] + from_left[e, 2] + from_right[e, 1]
        unit[e, b_half] = ab[e, x, b_half] + from_left[e, 1] + from_right[e, 2]

    group8, quarter = z // 8, (z % 8) // 2
    their = jnp.where(z % 2 == 0, core, 1 - core)
    me = x * NH + h

    def strip(e, k):
        ox, oz = 2 * (1 - low) + their, group8 * 8 + quarter * 2 + k
        own = jnp.logical_and(ox == x, jnp.logical_and(h == e, oz == z))
        return own, device(ox, e, oz, low, core)

    def cross_out(e):
        block = unit_last(e)
        flip[e, 0, 0:32, :] = block
        column = lax.broadcasted_iota(jnp.int32, (TILE, TILE), 1)
        tall = jnp.concatenate([block] * 4, axis=0).T
        flip[e, 1] = jnp.where(column // 32 == quarter, tall, 0.0)
        wide = pl.ds(pl.multiple_of((2 * e + group8) * TILE, TILE), TILE)
        lanes = pl.ds(pl.multiple_of(x * TILE, TILE), TILE)

        @pl.loop(0, 8)
        def _(k):
            src = pl.ds(pl.multiple_of(k * 16, 16), 16)
            pltpu.make_async_remote_copy(
                src_ref=flip.at[e, 1, src], dst_ref=turned.at[quarter * 2 + h, :, wide],
                send_sem=fin_ss.at[e, 2 + k], recv_sem=fin_rs.at[1],
                device_id=device(2 * low + core, x // 2, (x % 2) * 8 + k, 1 - low, their),
                device_id_type=MESH,
            ).start()

        for k in range(2):
            src = pl.ds(k * 16, 16)
            own, owner = strip(e, k)

            @pl.when(own)
            def _():
                pltpu.make_async_copy(flip.at[e, 0, src], direct.at[h, :, lanes], fin_rs.at[0]).start()

            @pl.when(jnp.logical_not(own))
            def _():
                pltpu.make_async_remote_copy(
                    src_ref=flip.at[e, 0, src], dst_ref=direct.at[h, :, lanes],
                    send_sem=fin_ss.at[e, k], recv_sem=fin_rs.at[0],
                    device_id=owner, device_id_type=MESH,
                ).start()

    def other_chip():
        arrived(other, core_rs)
        for q in range(ROWS // TILE):
            rows = slice(q * TILE, (q + 1) * TILE)
            for j in range(4):
                turn(other[rows, j * TILE:(j + 1) * TILE] - mean[rows, :], q, t_hi.at[1], t_lo.at[1], j)

    own_chip(0)
    own_step(0, 0)
    relay(0, 0)
    other_chip()
    e_step(1)
    relay(0, 1)
    own_step(0, 1)
    own_chip(1)
    own_step(1, 0)
    e_step(2)
    relay(0, 2)
    own_step(0, 2)
    turn_cross(0, 0, 0)
    turn_cross(0, 0, 1)
    turn_cross(0, 0, 2)
    turn_cross(1, 0, 0)
    turn_cross(1, 0, 1)
    turn_cross(1, 0, 2)
    cross_chip(0)
    x_first(0)
    own_step(1, 1)
    own_step(0, 3)
    relay(1, 0)
    turn_cross(0, 1, 0)
    relay(1, 1)
    e_step(3)
    own_step(1, 2)
    turn_cross(0, 1, 1)
    turn_cross(1, 1, 0)
    turn_cross(1, 1, 1)
    own_step(0, 4)
    x_second(0)
    relay(1, 2)
    turn_cross(0, 1, 2)
    turn_cross(1, 1, 2)
    cross_chip(1)
    x_first(1)
    own_step(1, 3)
    own_step(0, 5)
    x_last(0)
    unit_step(0, 0)
    own_step(1, 4)
    x_second(1)
    own_step(0, 6)
    unit_step(0, 1)
    e_step(4)
    own_step(1, 5)
    own_step(0, 7)
    unit_step(0, 2)
    x_last(1)
    unit_step(1, 0)
    own_step(1, 6)
    unit_step(0, 3)
    e_step(5)
    unit_step(1, 1)
    own_step(1, 7)
    cross_out(0)
    unit_step(1, 2)
    e_step(6)
    own_out()
    unit_step(1, 3)
    cross_out(1)
    e_step(7)

    line = h * 2 + z // 8
    e_col[...] = jnp.broadcast_to(e_all[x, pl.ds(line, 1), :], (TILE, TILE)).T
    scale_j = lax.rsqrt(e_col[pl.ds(pl.multiple_of((z % 8) * 16, 16), 16), :] + eps)
    scale_i = lax.rsqrt(e_all[s] + eps)

    def finish(total):
        for j in range(4):
            lanes = slice(j * TILE, (j + 1) * TILE)
            out_ref[:, lanes] = total[:, lanes] * scale_i[j:j + 1, :] * scale_j

    for src, sem in pending:
        arrived(src, sem)

    @pl.when(x // 2 == low)
    def _():
        arrived(direct, fin_rs.at[0])
        finish(jnp.sum(direct[...], axis=0))

    @pl.when(x // 2 != low)
    def _():
        arrived(direct.at[pl.ds(0, 2)], fin_rs.at[0])
        arrived(turned, fin_rs.at[1])
        finish(direct[0] + direct[1] + jnp.sum(turned[...], axis=0))

    for u in range(4):
        mine, _ = own_owner(u)

        @pl.when(jnp.logical_not(mine))
        def _():
            arrived(held.at[u], own_ss.at[u])

    for e in range(2):
        src = flip.at[e, 0, pl.ds(0, 16)]
        for k in range(2):
            own, _ = strip(e, k)

            @pl.when(jnp.logical_not(own))
            def _():
                arrived(src, fin_ss.at[e, k])

        @pl.loop(0, 8)
        def _(k):
            arrived(src, fin_ss.at[e, 2 + k])


def per_device(snapshots):
    dma = pltpu.SemaphoreType.DMA
    vmem = pltpu.VMEM
    strip = pl.pallas_call(
        kernel,
        out_shape=jax.ShapeDtypeStruct((16, COLS), f32),
        in_specs=[pl.BlockSpec(memory_space=pl.ANY)],
        out_specs=pl.BlockSpec(memory_space=pltpu.VMEM),
        scratch_shapes=[
            vmem((ROWS, COLS), f32), vmem((ROWS, COLS), f32),
            vmem((2, HALF, COLS), f32),
            vmem((4, 8, TILE), f32),
            vmem((ROWS, TILE), f32),
            vmem((ROWS, COLS), bf16), vmem((ROWS, COLS), bf16),
            vmem((2, COLS, ROWS), bf16), vmem((2, COLS, ROWS), bf16),
            vmem((2, COLS, HALF), bf16), vmem((2, COLS, HALF), bf16),
            vmem((NZ, 4, 16, COLS), f32),
            vmem((2, NX, NZ, 32, TILE), f32),
            vmem((2, NZ, 32, TILE), f32),
            vmem((2, 3, ZR, 32, TILE), f32), vmem((2, 3, ZR, 32, TILE), f32),
            vmem((2, 4, 32, TILE), f32), vmem((2, 4, 32, TILE), f32),
            vmem((2, 4, 32, TILE), f32), vmem((2, 3, 32, TILE), f32),
            vmem((SUB, ZR, WIDE, 16, COLS), f32), vmem((SUB, ZL, WIDE, 16, COLS), f32),
            vmem((8, TILE), f32), vmem((3, 8, TILE), f32),
            vmem((4, 8, TILE), f32), vmem((6, 8, TILE), f32),
            vmem((4, 8, TILE), f32), vmem((TILE, TILE), f32),
            vmem((4, 16, COLS), f32), vmem((2, 2, TILE, TILE), f32),
            vmem((8, 16, COLS), f32), vmem((8, 16, COLS), f32),
            dma((6,)), dma, dma, dma((2, 3)), dma((2, 3)), dma((2, 3)), dma((2, 3)), dma((3,)), dma((3,)),
            dma((2, 3)), dma((2, 3)), dma((2, 3)), dma((2, 3)),
            dma((2, 4)), dma((2, 4)), dma((2, 4)), dma((2, 4)), dma((2, 4)), dma((2, 4)), dma((2, 3)), dma((2, 3)),
            dma((SUB, ZR)), dma((SUB, ZR)), dma((SUB, ZL)), dma((SUB, ZL)),
            dma((3,)), dma((3,)), dma((6,)), dma((6,)), dma((3,)), dma((3,)),
            dma((4,)), dma((2, 10)), dma((2,)),
        ],
        compiler_params=pltpu.CompilerParams(
            collective_id=0, has_side_effects=True, vmem_limit_bytes=48 << 20
        ),
        cost_estimate=pl.CostEstimate(flops=3_600_000_000, bytes_accessed=1_700_000, transcendentals=0),
        name="gram",
    )(snapshots)
    return strip.T


def solution(mesh):
    return jax.shard_map(
        per_device, mesh=mesh, in_specs=(P("rows", "snap"),), out_specs=P("snap", "rows"), check_vma=False
    )
```

```python
import jax
import jax.numpy as jnp
from jax import lax
from jax.experimental import pallas as pl
from jax.experimental.pallas import tpu as pltpu
from jax.sharding import PartitionSpec as P

eps = 1e-06
MESH = pl.DeviceIdType.MESH
f32, bf16 = jnp.float32, jnp.bfloat16

NX, NH, NZ = 4, 2, 16
ROWS, COLS = 768, 512
HALF = ROWS // 2
TILE = 128
SNAPS = 2048
SUB = 2
WIDE = 4 // SUB
ZR, ZL = NZ // 2, NZ // 2 - 1


def device(x, h, z, low, core):
    return ((x * NH + h) * NZ + z, low * 2 + core)


def kernel(
    x_hbm, out_ref,
    x_ref, other, cross, sums, mean, hi, lo, t_hi, t_lo, c_hi, c_lo,
    aa, ab, unit, from_left, from_right,
    unit_re, unit_ro, unit_lo, unit_le, aa_r, aa_l,
    e_own, e_x, e_z, e_g, e_all, e_col,
    held, flip, direct, turned,
    in_sem, core_ss, core_rs, y_ss, y_rs, relay_ss, relay_rs, sum_ss, sum_rs,
    xr_ss, xr_rs, xl_ss, xl_rs,
    ure_ss, ure_rs, uro_ss, uro_rs, ulo_ss, ulo_rs, ule_ss, ule_rs, aar_ss, aar_rs, aal_ss, aal_rs,
    ex_ss, ex_rs, ez_ss, ez_rs, eg_ss, eg_rs,
    own_ss, fin_ss, fin_rs,
):
    r, s = lax.axis_index("rows"), lax.axis_index("snap")
    x, h, z = r // (NH * NZ), (r // NZ) % NH, r % NZ
    low, core = s // 2, s % 2
    zr, zl = device(x, h, (z + 1) % NZ, low, core), device(x, h, (z + NZ - 1) % NZ, low, core)
    zr2, zl2 = device(x, h, (z + 2) % NZ, low, core), device(x, h, (z + NZ - 2) % NZ, low, core)
    xr, xl = device((x + 1) % NX, h, z, low, core), device((x + NX - 1) % NX, h, z, low, core)
    xx = device((x + 2) % NX, h, z, low, core)
    hh = device(x, 1 - h, z, low, core)
    twin = device(x, h, z, low, 1 - core)
    pair = device(x, h, z, 1 - low, core)
    diagonal = device(x, h, z, 1 - low, 1 - core)
    group = (twin, pair, diagonal)
    pending = []

    def send(src, dst, send_sem, recv_sem, target):
        copy = pltpu.make_async_remote_copy(
            src_ref=src, dst_ref=dst, send_sem=send_sem, recv_sem=recv_sem,
            device_id=target, device_id_type=MESH,
        )
        copy.start()
        pending.append((src, send_sem))
        return copy

    def arrived(dst, sem):
        pltpu.make_async_copy(dst, dst, sem).wait()

    def load(q):
        rows = pl.ds(q * TILE, TILE)
        return pltpu.make_async_copy(x_hbm.at[rows], x_ref.at[rows], in_sem.at[q])

    for q in range(ROWS // TILE):
        load(q).start()
    barrier = pltpu.get_barrier_semaphore()
    near = (twin, pair, diagonal, zr, zl, zr2, zl2, xr, xl, xx, hh)
    for target in near:
        pl.semaphore_signal(barrier, inc=1, device_id=target, device_id_type=MESH)

    def row_sums(q):
        load(q).wait()
        block = x_ref[q * TILE:(q + 1) * TILE, :]
        part = block[:, 0:128] + block[:, 128:256] + block[:, 256:384] + block[:, 384:512]
        sums[s, q:q + 1, :] = jnp.sum(part.T, axis=0, keepdims=True)

    for q in range(ROWS // TILE):
        row_sums(q)
    sums[s, 6:8, :] = jnp.zeros((2, TILE), f32)
    pl.semaphore_wait(barrier, len(near))

    for i, target in enumerate(group):
        send(sums.at[s], sums.at[s], sum_ss.at[i], sum_rs.at[i], target)
    give = pl.multiple_of((1 - low) * HALF, HALF)
    for e in range(2):
        for q in range(HALF // TILE):
            lanes = pl.ds(e * 256, 256)
            send(x_ref.at[pl.ds(give + q * TILE, TILE), lanes], cross.at[0, pl.ds(q * TILE, TILE), lanes],
                 y_ss.at[e, q], y_rs.at[e, q], pair)
        if e == 0:
            send(x_ref, other, core_ss, core_rs, twin)

    for i, d in enumerate((s ^ 1, s ^ 2, s ^ 3)):
        arrived(sums.at[d], sum_rs.at[i])
    mean_rows = (sums[0] + sums[1] + sums[2] + sums[3]) / SNAPS
    for q in range(ROWS // TILE):
        wide = jnp.broadcast_to(mean_rows[q:q + 1, :], (TILE, TILE))
        mean[q * TILE:(q + 1) * TILE, :] = wide.T

    def split(value):
        high = value.astype(bf16)
        return high, (value - high.astype(f32)).astype(bf16)

    def turn(block, q, to_hi, to_lo, j):
        high, rest = split(block.T)
        to_hi[j * TILE:(j + 1) * TILE, q * TILE:(q + 1) * TILE] = high
        to_lo[j * TILE:(j + 1) * TILE, q * TILE:(q + 1) * TILE] = rest

    energy = [jnp.zeros((8, TILE), f32) for _ in range(4)]
    for q in range(ROWS // TILE):
        rows = slice(q * TILE, (q + 1) * TILE)
        for j in range(4):
            block = x_ref[rows, j * TILE:(j + 1) * TILE] - mean[rows, :]
            energy[j] += jnp.sum((block * block).reshape(TILE // 8, 8, TILE), axis=0)
            high, rest = split(block)
            hi[rows, j * TILE:(j + 1) * TILE] = high
            lo[rows, j * TILE:(j + 1) * TILE] = rest
            turn(block, q, t_hi.at[0], t_lo.at[0], j)
    for j in range(4):
        e_own[j:j + 1, :] = jnp.sum(energy[j], axis=0, keepdims=True)
    e_own[4:8, :] = jnp.zeros((4, TILE), f32)

    z1 = device(x, h, z + 1 - 2 * (z % 2), low, core)
    z2 = device(x, h, z + 2 - 4 * ((z // 2) % 2), low, core)
    z4r, z4l = device(x, h, (z + 4) % NZ, low, core), device(x, h, (z + NZ - 4) % NZ, low, core)

    def e_step(t):
        if t == 0:
            send(e_own, e_g.at[0], ez_ss.at[0], ez_rs.at[0], z1)
        elif t == 1:
            arrived(e_g.at[0], ez_rs.at[0])
            e_z[0] = e_own[...] + e_g[0]
            send(e_z.at[0], e_g.at[1], ez_ss.at[1], ez_rs.at[1], z2)
        elif t == 2:
            arrived(e_g.at[1], ez_rs.at[1])
            e_z[1] = e_z[0] + e_g[1]
            for i, target in enumerate((xr, xl, xx)):
                send(e_z.at[1], e_x.at[i], ex_ss.at[i], ex_rs.at[i], target)
        elif t == 3:
            for i in range(3):
                arrived(e_x.at[i], ex_rs.at[i])
            e_z[2] = e_z[1] + e_x[0] + e_x[1] + e_x[2]
            send(e_z.at[2], e_g.at[2], ez_ss.at[2], ez_rs.at[2], hh)
        elif t == 4:
            arrived(e_g.at[2], ez_rs.at[2])
            e_z[3] = e_z[2] + e_g[2]
            send(e_z.at[3], e_g.at[3], ez_ss.at[3], ez_rs.at[3], z4r)
            send(e_z.at[3], e_g.at[4], ez_ss.at[4], ez_rs.at[4], z4l)
        elif t == 5:
            arrived(e_g.at[3], ez_rs.at[3])
            send(e_g.at[3], e_g.at[5], ez_ss.at[5], ez_rs.at[5], z4r)
            arrived(e_g.at[4], ez_rs.at[4])
        elif t == 6:
            arrived(e_g.at[5], ez_rs.at[5])
            e_all[s] = e_z[3] + e_g[3] + e_g[4] + e_g[5]
            for i, target in enumerate(group):
                send(e_all.at[s], e_all.at[s], eg_ss.at[i], eg_rs.at[i], target)
        else:
            for i, d in enumerate((s ^ 1, s ^ 2, s ^ 3)):
                arrived(e_all.at[d], eg_rs.at[i])

    e_step(0)

    def product(a_hi, a_lo, b_hi, b_lo):
        total = jnp.dot(a_hi, b_hi, preferred_element_type=f32)
        total += jnp.dot(a_hi, b_lo, preferred_element_type=f32)
        return total + jnp.dot(a_lo, b_hi, preferred_element_type=f32)

    def own_chip(side):
        got = product(t_hi[side], t_lo[side], hi[...], lo[...])
        for half in range(2):
            aa[:, side * 2 + half] = got[half * 256:(half + 1) * 256].reshape(NZ, 16, COLS)

    keep = pl.multiple_of(low * HALF, HALF)

    def relay(e, q):
        piece = (pl.ds(q * TILE, TILE), pl.ds(e * 256, 256))
        arrived(cross.at[(0,) + piece], y_rs.at[e, q])
        send(cross.at[(0,) + piece], cross.at[(1,) + piece], relay_ss.at[e, q], relay_rs.at[e, q], twin)

    def turn_cross(side, e, q):
        if side == 1:
            arrived(cross.at[1, pl.ds(q * TILE, TILE), pl.ds(e * 256, 256)], relay_rs.at[e, q])
        rows = slice(q * TILE, (q + 1) * TILE)
        level = mean[pl.ds(keep + q * TILE, TILE), :]
        for g in range(2):
            lanes = slice((2 * e + g) * TILE, (2 * e + g + 1) * TILE)
            turn(cross[side, rows, lanes] - level, q, c_hi.at[e], c_lo.at[e], side * 2 + g)

    def cross_chip(e):
        got = product(c_hi[e], c_lo[e], hi[pl.ds(keep, HALF), :], lo[pl.ds(keep, HALF), :])
        for side in range(2):
            for g in range(2):
                for j in range(4):
                    for k in range(4):
                        at = (side * 2 + g) * TILE + k * 32
                        ab[e, j, 8 * g + 2 * k + side] = got[at:at + 32, j * TILE:(j + 1) * TILE]

    def hop(t, part, slots, ss, rs, target):
        src = part if t == 0 else slots.at[t - 1]
        if t > 0:
            arrived(slots.at[t - 1], rs.at[t - 1])
            slots[t - 1] = slots[t - 1] + part[...]
        send(src, slots.at[t], ss.at[t], rs.at[t], target)

    def unit_step(e, t):
        def one(distance, slots, ss, rs, target):
            hop(t, unit.at[e, (z + distance) % NZ], slots.at[e], ss.at[e], rs.at[e], target)

        one(8 - 2 * t, unit_re, ure_ss, ure_rs, zr2)
        one(9 + 2 * t, unit_lo, ulo_ss, ulo_rs, zl2 if t < 3 else zl)
        one(7 - 2 * t, unit_ro, uro_ss, uro_rs, zr2 if t < 3 else zr)
        if t < 3:
            one(10 + 2 * t, unit_le, ule_ss, ule_rs, zl2)

    def unit_last(e):
        total = unit[e, z]
        for slots, rs, n in ((unit_le, ule_rs, 3), (unit_re, ure_rs, 4), (unit_ro, uro_rs, 4), (unit_lo, ulo_rs, 4)):
            arrived(slots.at[e, n - 1], rs.at[e, n - 1])
            total = total + slots[e, n - 1]
        return total

    def own_step(u, t):
        half = pl.ds(WIDE * u, WIDE)
        if t < ZR:
            hop(t, aa.at[(z + ZR - t) % NZ, half], aa_r.at[u], aar_ss.at[u], aar_rs.at[u], zr)
        if t < ZL:
            hop(t, aa.at[(z + NZ - ZL + t) % NZ, half], aa_l.at[u], aal_ss.at[u], aal_rs.at[u], zl)

    def own_owner(u):
        ox, oh = 2 * low + (core if u < 2 else 1 - core), u % 2
        return jnp.logical_and(ox == x, oh == h), device(ox, oh, z, low, core)

    def own_out():
        for u in range(SUB):
            arrived(aa_r.at[u, ZR - 1], aar_rs.at[u, ZR - 1])
            arrived(aa_l.at[u, ZL - 1], aal_rs.at[u, ZL - 1])
            half = pl.ds(WIDE * u, WIDE)
            held[half] = aa[z, half] + aa_r[u, ZR - 1] + aa_l[u, ZL - 1]
        for u in range(4):
            mine, owner = own_owner(u)

            @pl.when(mine)
            def _():
                pltpu.make_async_copy(held.at[u], direct.at[me], fin_rs.at[0]).start()

            @pl.when(jnp.logical_not(mine))
            def _():
                pltpu.make_async_remote_copy(
                    src_ref=held.at[u], dst_ref=direct.at[me], send_sem=own_ss.at[u], recv_sem=fin_rs.at[0],
                    device_id=owner, device_id_type=MESH,
                ).start()

    a_half, b_half = pl.ds(0, ZR), pl.ds(ZR, ZR)
    far, right, left = (x + 2) % NX, (x + 1) % NX, (x + NX - 1) % NX

    def x_first(e):
        part, by_l, by_r = ab.at[e], from_left.at[e], from_right.at[e]
        send(part.at[far, a_half], by_l.at[0], xr_ss.at[e, 0], xr_rs.at[e, 0], xr)
        send(part.at[far, b_half], by_r.at[0], xl_ss.at[e, 0], xl_rs.at[e, 0], xl)
        send(part.at[right, b_half], by_l.at[1], xr_ss.at[e, 1], xr_rs.at[e, 1], xr)
        send(part.at[left, a_half], by_r.at[1], xl_ss.at[e, 1], xl_rs.at[e, 1], xl)

    def x_second(e):
        part, by_l, by_r = ab.at[e], from_left.at[e], from_right.at[e]
        arrived(by_l.at[0], xr_rs.at[e, 0])
        by_l[0] = by_l[0] + part[right, a_half]
        send(by_l.at[0], by_l.at[2], xr_ss.at[e, 2], xr_rs.at[e, 2], xr)
        arrived(by_r.at[0], xl_rs.at[e, 0])
        by_r[0] = by_r[0] + part[left, b_half]
        send(by_r.at[0], by_r.at[2], xl_ss.at[e, 2], xl_rs.at[e, 2], xl)

    def x_last(e):
        for i in (1, 2):
            arrived(from_left.at[e, i], xr_rs.at[e, i])
            arrived(from_right.at[e, i], xl_rs.at[e, i])
        unit[e, a_half] = ab[e, x, a_half] + from_left[e, 2] + from_right[e, 1]
        unit[e, b_half] = ab[e, x, b_half] + from_left[e, 1] + from_right[e, 2]

    group8, quarter = z // 8, (z % 8) // 2
    their = jnp.where(z % 2 == 0, core, 1 - core)
    me = x * NH + h

    def strip(e, k):
        ox, oz = 2 * (1 - low) + their, group8 * 8 + quarter * 2 + k
        own = jnp.logical_and(ox == x, jnp.logical_and(h == e, oz == z))
        return own, device(ox, e, oz, low, core)

    def cross_out(e):
        block = unit_last(e)
        flip[e, 0, 0:32, :] = block
        column = lax.broadcasted_iota(jnp.int32, (TILE, TILE), 1)
        tall = jnp.concatenate([block] * 4, axis=0).T
        flip[e, 1] = jnp.where(column // 32 == quarter, tall, 0.0)
        wide = pl.ds(pl.multiple_of((2 * e + group8) * TILE, TILE), TILE)
        lanes = pl.ds(pl.multiple_of(x * TILE, TILE), TILE)

        for k in range(8):
            src = pl.ds(k * 16, 16)
            pltpu.make_async_remote_copy(
                src_ref=flip.at[e, 1, src], dst_ref=turned.at[quarter * 2 + h, :, wide],
                send_sem=fin_ss.at[e, 2 + k], recv_sem=fin_rs.at[1],
                device_id=device(2 * low + core, x // 2, (x % 2) * 8 + k, 1 - low, their),
                device_id_type=MESH,
            ).start()

        for k in range(2):
            src = pl.ds(k * 16, 16)
            own, owner = strip(e, k)

            @pl.when(own)
            def _():
                pltpu.make_async_copy(flip.at[e, 0, src], direct.at[h, :, lanes], fin_rs.at[0]).start()

            @pl.when(jnp.logical_not(own))
            def _():
                pltpu.make_async_remote_copy(
                    src_ref=flip.at[e, 0, src], dst_ref=direct.at[h, :, lanes],
                    send_sem=fin_ss.at[e, k], recv_sem=fin_rs.at[0],
                    device_id=owner, device_id_type=MESH,
                ).start()

    def other_chip():
        arrived(other, core_rs)
        for q in range(ROWS // TILE):
            rows = slice(q * TILE, (q + 1) * TILE)
            for j in range(4):
                turn(other[rows, j * TILE:(j + 1) * TILE] - mean[rows, :], q, t_hi.at[1], t_lo.at[1], j)

    own_chip(0)
    own_step(0, 0)
    relay(0, 0)
    other_chip()
    e_step(1)
    relay(0, 1)
    own_step(0, 1)
    own_chip(1)
    own_step(1, 0)
    e_step(2)
    relay(0, 2)
    own_step(0, 2)
    turn_cross(0, 0, 0)
    turn_cross(0, 0, 1)
    turn_cross(0, 0, 2)
    turn_cross(1, 0, 0)
    turn_cross(1, 0, 1)
    turn_cross(1, 0, 2)
    cross_chip(0)
    x_first(0)
    own_step(1, 1)
    own_step(0, 3)
    relay(1, 0)
    turn_cross(0, 1, 0)
    relay(1, 1)
    e_step(3)
    own_step(1, 2)
    turn_cross(0, 1, 1)
    turn_cross(1, 1, 0)
    turn_cross(1, 1, 1)
    own_step(0, 4)
    x_second(0)
    relay(1, 2)
    turn_cross(0, 1, 2)
    turn_cross(1, 1, 2)
    cross_chip(1)
    x_first(1)
    own_step(1, 3)
    own_step(0, 5)
    x_last(0)
    unit_step(0, 0)
    own_step(1, 4)
    x_second(1)
    own_step(0, 6)
    unit_step(0, 1)
    e_step(4)
    own_step(1, 5)
    own_step(0, 7)
    unit_step(0, 2)
    x_last(1)
    unit_step(1, 0)
    own_step(1, 6)
    unit_step(0, 3)
    e_step(5)
    unit_step(1, 1)
    own_step(1, 7)
    cross_out(0)
    unit_step(1, 2)
    e_step(6)
    own_out()
    unit_step(1, 3)
    cross_out(1)
    e_step(7)

    line = h * 2 + z // 8
    e_col[...] = jnp.broadcast_to(e_all[x, pl.ds(line, 1), :], (TILE, TILE)).T
    scale_j = lax.rsqrt(e_col[pl.ds(pl.multiple_of((z % 8) * 16, 16), 16), :] + eps)
    scale_i = lax.rsqrt(e_all[s] + eps)

    def finish(total):
        for j in range(4):
            lanes = slice(j * TILE, (j + 1) * TILE)
            out_ref[:, lanes] = total[:, lanes] * scale_i[j:j + 1, :] * scale_j

    for src, sem in pending:
        arrived(src, sem)

    @pl.when(x // 2 == low)
    def _():
        arrived(direct, fin_rs.at[0])
        finish(jnp.sum(direct[...], axis=0))

    @pl.when(x // 2 != low)
    def _():
        arrived(direct.at[pl.ds(0, 2)], fin_rs.at[0])
        arrived(turned, fin_rs.at[1])
        finish(direct[0] + direct[1] + jnp.sum(turned[...], axis=0))

    for u in range(4):
        mine, _ = own_owner(u)

        @pl.when(jnp.logical_not(mine))
        def _():
            arrived(held.at[u], own_ss.at[u])

    for e in range(2):
        src = flip.at[e, 0, pl.ds(0, 16)]
        for k in range(2):
            own, _ = strip(e, k)

            @pl.when(jnp.logical_not(own))
            def _():
                arrived(src, fin_ss.at[e, k])

        for k in range(8):
            arrived(src, fin_ss.at[e, 2 + k])


def per_device(snapshots):
    dma = pltpu.SemaphoreType.DMA
    vmem = pltpu.VMEM
    strip = pl.pallas_call(
        kernel,
        out_shape=jax.ShapeDtypeStruct((16, COLS), f32),
        in_specs=[pl.BlockSpec(memory_space=pl.ANY)],
        out_specs=pl.BlockSpec(memory_space=pltpu.VMEM),
        scratch_shapes=[
            vmem((ROWS, COLS), f32), vmem((ROWS, COLS), f32),
            vmem((2, HALF, COLS), f32),
            vmem((4, 8, TILE), f32),
            vmem((ROWS, TILE), f32),
            vmem((ROWS, COLS), bf16), vmem((ROWS, COLS), bf16),
            vmem((2, COLS, ROWS), bf16), vmem((2, COLS, ROWS), bf16),
            vmem((2, COLS, HALF), bf16), vmem((2, COLS, HALF), bf16),
            vmem((NZ, 4, 16, COLS), f32),
            vmem((2, NX, NZ, 32, TILE), f32),
            vmem((2, NZ, 32, TILE), f32),
            vmem((2, 3, ZR, 32, TILE), f32), vmem((2, 3, ZR, 32, TILE), f32),
            vmem((2, 4, 32, TILE), f32), vmem((2, 4, 32, TILE), f32),
            vmem((2, 4, 32, TILE), f32), vmem((2, 3, 32, TILE), f32),
            vmem((SUB, ZR, WIDE, 16, COLS), f32), vmem((SUB, ZL, WIDE, 16, COLS), f32),
            vmem((8, TILE), f32), vmem((3, 8, TILE), f32),
            vmem((4, 8, TILE), f32), vmem((6, 8, TILE), f32),
            vmem((4, 8, TILE), f32), vmem((TILE, TILE), f32),
            vmem((4, 16, COLS), f32), vmem((2, 2, TILE, TILE), f32),
            vmem((8, 16, COLS), f32), vmem((8, 16, COLS), f32),
            dma((6,)), dma, dma, dma((2, 3)), dma((2, 3)), dma((2, 3)), dma((2, 3)), dma((3,)), dma((3,)),
            dma((2, 3)), dma((2, 3)), dma((2, 3)), dma((2, 3)),
            dma((2, 4)), dma((2, 4)), dma((2, 4)), dma((2, 4)), dma((2, 4)), dma((2, 4)), dma((2, 3)), dma((2, 3)),
            dma((SUB, ZR)), dma((SUB, ZR)), dma((SUB, ZL)), dma((SUB, ZL)),
            dma((3,)), dma((3,)), dma((6,)), dma((6,)), dma((3,)), dma((3,)),
            dma((4,)), dma((2, 10)), dma((2,)),
        ],
        compiler_params=pltpu.CompilerParams(
            collective_id=0, has_side_effects=True, vmem_limit_bytes=48 << 20
        ),
        cost_estimate=pl.CostEstimate(flops=3_600_000_000, bytes_accessed=1_700_000, transcendentals=0),
        name="gram",
    )(snapshots)
    return strip.T


def solution(mesh):
    return jax.shard_map(
        per_device, mesh=mesh, in_specs=(P("rows", "snap"),), out_specs=P("snap", "rows"), check_vma=False
    )
```
